32 devices in a mesh: ctx: 16 (over z, y, core), head: 2 (over x).
Axes of the slice: x: 2, y: 2, z: 4, core: 2. Of those that a mesh axis runs over, the one named last changes fastest.
Arguments:
- prompt_latent: bfloat16 [1536, 576], P('ctx'), may hold values from -8 to 8
- prefill_query: bfloat16 [1024, 64, 192], P('ctx', 'head'), may hold values from -12 to 12
- span_start: int32 [1], replicated, may hold values from 0 to 512
- w_uk: bfloat16 [64, 128, 512], P('head'), may hold values from -0.5 to 0.5
- w_uv: bfloat16 [64, 512, 128], P('head'), may hold values from -0.25 to 0.25
- decode_latent: bfloat16 [64, 64, 576], P(None, 'ctx'), may hold values from -8 to 8
- owner_slot: int32 [64], replicated, may hold values from 0 to 63, each once
- lengths: int32 [64], P('ctx'), may hold values from 1 to 64
- hidden_new: bfloat16 [4, 64, 7168], P(None, 'ctx', 'head'), may hold values from -6 to 6
- decode_query: bfloat16 [4, 64, 64, 192], P(None, 'ctx', 'head'), may hold values from -12 to 12
- w_down: bfloat16 [7168, 576], P('head'), may hold values from -0.0625 to 0.0625
- kv_gain: float32 [512], replicated, may hold values from 0.5 to 1.5
Outputs:
- prefill_out: bfloat16 [1024, 64, 128], P('ctx', 'head')
- decode_out: bfloat16 [4, 64, 64, 128], P(None, 'ctx', 'head')
The draws below stay inside these ranges and needn't reach their ends.
Inputs may be any that keep to these rules, and one draw needn't show every extreme that they name: span_start + 1024 <= 1536. `owner_slot`: each slot once.
All inputs are finite; a program needn't handle non-finite values.
Results may differ from the reference program's by a relative error of at most 0.014.
Values may be sent and summed in bfloat16 or wider, within the bound.
A program may use at most 128 MiB of HBM per device.

```python
import jax
import jax.numpy as jnp
from jax import lax

D = 7168
HEADS = 64
KV_RANK = 512
ROPE = 64
NOPE = 128
VDIM = 128
STEPS = 4
LAT = 576
CTX = 1536
QTOK = 1024
CAP = 64
REQS = 64


def base_draw(key, shape):
    values = jax.random.truncated_normal(key, -6.0, 6.0, shape, jnp.float32)
    return values


def draw_prompt_latent(key, part):
    values = base_draw(jax.random.fold_in(key, 11), (CTX, LAT))
    return values.astype(jnp.bfloat16)


def draw_decode_latent(key, part):
    values = base_draw(jax.random.fold_in(key, 13), (REQS, CAP, LAT))
    return values.astype(jnp.bfloat16)


def draw_prefill_query(key, part):
    values = base_draw(jax.random.fold_in(key, 12), (QTOK, HEADS, NOPE + ROPE))
    return values.astype(jnp.bfloat16)


def draw_decode_query(key, part):
    values = base_draw(jax.random.fold_in(key, 14), (STEPS, REQS, HEADS, NOPE + ROPE))
    return values.astype(jnp.bfloat16)


def set_ends(entries, key, low, high):
    longest = entries.shape.index(max(entries.shape))
    spots = []
    for shift in (0, 1):
        where = [jax.random.randint(jax.random.fold_in(key, axis), (), 0, length) for axis, length in enumerate(entries.shape)]
        where[longest] = (where[longest] + shift) % entries.shape[longest]
        spots.append(tuple(where))
    return entries.at[spots[0]].set(low).at[spots[1]].set(high)


def shard_levels(own_key, shape, pieces, least, top_value):
    def one(position, parts):
        steps = jax.random.uniform(jax.random.fold_in(jax.random.fold_in(own_key, 6), position), (parts,), jnp.float32, least / len(pieces), top_value / len(pieces))
        return jnp.repeat(jnp.exp(steps), shape[position] // parts).reshape((-1,) + (1,) * (len(shape) - position - 1))

    gain = one(*pieces[0])
    for cut in pieces[1:]:
        gain = gain * one(*cut)
    return gain


def normal_values(stream_key, extent, deviation, bound, cuts=(), kind=jnp.bfloat16):
    entries = deviation * jax.random.normal(stream_key, extent, jnp.float32)
    if cuts:
        entries = entries * shard_levels(stream_key, extent, cuts, -0.22, 0.18)
    return jnp.clip(entries, -bound, bound).astype(kind)


def setup_inputs(seed: int = 0) -> dict:
    seeds = jax.random.split(jax.random.key(seed), 13)
    return {
        "prompt_latent": draw_prompt_latent(jax.random.fold_in(seeds[12], 71), 0),
        "prefill_query": draw_prefill_query(jax.random.fold_in(seeds[12], 71), 0),
        "span_start": jax.random.randint(seeds[2], (1,), 0, CTX - QTOK + 1).astype(jnp.int32),
        "w_uk": normal_values(seeds[3], (HEADS, NOPE, KV_RANK), NOPE ** -0.5, 0.5, ((0, 2),)),
        "w_uv": normal_values(seeds[4], (HEADS, KV_RANK, VDIM), KV_RANK ** -0.5, 0.25, ((0, 2),)),
        "decode_latent": draw_decode_latent(jax.random.fold_in(seeds[12], 71), 0),
        "owner_slot": jax.random.permutation(seeds[6], REQS).astype(jnp.int32),
        "lengths": set_ends(jax.random.randint(seeds[7], (REQS,), 1, CAP + 1), jax.random.fold_in(seeds[7], 1), 1, CAP).astype(jnp.int32),
        "hidden_new": normal_values(seeds[8], (STEPS, REQS, D), 1.0, 6.0, ((1, 16), (2, 2))),
        "decode_query": draw_decode_query(jax.random.fold_in(seeds[12], 71), 0),
        "w_down": normal_values(seeds[10], (D, LAT), D ** -0.5, 0.0625, ((0, 2),)),
        "kv_gain": jnp.clip(1.0 + 0.1 * jax.random.normal(seeds[11], (KV_RANK,), jnp.float32), 0.5, 1.5),
    }


def absorb(query, w_uk, form):
    nope = query[..., :NOPE].astype(jnp.float32)
    absorbed = jnp.einsum(form, nope, w_uk.astype(jnp.float32)).astype(jnp.bfloat16)
    return jnp.concatenate([absorbed, query[..., NOPE:]], axis=-1)

def reference(prompt_latent, prefill_query, span_start, w_uk, w_uv, decode_latent, owner_slot, lengths, hidden_new, decode_query, w_down, kv_gain):
    scale = (NOPE + ROPE) ** (-0.5)
    full_query = absorb(prefill_query, w_uk, 'qhn,hnc->qhc')
    positions = span_start[0] + jnp.arange(QTOK, dtype=jnp.int32)
    allowed = jnp.arange(CTX, dtype=jnp.int32)[None, :] <= positions[:, None]

    def one_head(items):
        rows, w_head = items
        scores = jnp.dot(rows, prompt_latent.T, preferred_element_type=jnp.float32) * scale
        peak = lax.optimization_barrier(jnp.max(jnp.where(allowed, scores, -1e+30), axis=1))
        probs = jnp.where(allowed, jnp.exp(scores - peak[:, None]), 0.0)
        total = lax.optimization_barrier(jnp.sum(probs, axis=1))
        mixed = jnp.dot(probs.astype(jnp.bfloat16), prompt_latent[:, :KV_RANK], preferred_element_type=jnp.float32)
        mixed = (mixed / total[:, None]).astype(jnp.bfloat16)
        return jnp.dot(mixed, w_head, preferred_element_type=jnp.float32).astype(jnp.bfloat16)
    per_head = lax.map(one_head, (jnp.transpose(full_query, (1, 0, 2)), w_uv))
    prefill_out = jnp.transpose(per_head, (1, 0, 2))
    order = jnp.argsort(owner_slot).astype(jnp.int32)
    cache = decode_latent[order]
    raw = jnp.dot(hidden_new.reshape(-1, D), w_down, preferred_element_type=jnp.float32)
    front = raw[:, :KV_RANK]
    factor = lax.rsqrt(lax.optimization_barrier(jnp.mean(front * front, axis=1)) + 1e-06)
    normed = front * factor[:, None] * kv_gain[None, :]
    new_latent = jnp.concatenate([normed, raw[:, KV_RANK:]], axis=1).astype(jnp.bfloat16).reshape(STEPS, REQS, -1)
    query = absorb(decode_query, w_uk, 'srhn,hnc->srhc').astype(jnp.float32)
    cache_f = cache.astype(jnp.float32)
    new_f = new_latent.astype(jnp.float32)
    cache_scores = jnp.einsum('srhc,rjc->srhj', query, cache_f) * scale
    new_scores = jnp.einsum('srhc,trc->srht', query, new_f) * scale
    cache_ok = (jnp.arange(CAP, dtype=jnp.int32)[None, :] < lengths[:, None])[None, :, None, :]
    steps_idx = jnp.arange(STEPS, dtype=jnp.int32)
    new_ok = (steps_idx[None, :] <= steps_idx[:, None])[:, None, None, :]
    peak = jnp.maximum(lax.optimization_barrier(jnp.max(jnp.where(cache_ok, cache_scores, -1e+30), axis=3)), lax.optimization_barrier(jnp.max(jnp.where(new_ok, new_scores, -1e+30), axis=3)))
    cache_p = jnp.where(cache_ok, jnp.exp(cache_scores - peak[..., None]), 0.0)
    new_p = jnp.where(new_ok, jnp.exp(new_scores - peak[..., None]), 0.0)
    total = lax.optimization_barrier(jnp.sum(cache_p, axis=3)) + lax.optimization_barrier(jnp.sum(new_p, axis=3))
    cache_w = cache_p.astype(jnp.bfloat16).astype(jnp.float32)
    new_w = new_p.astype(jnp.bfloat16).astype(jnp.float32)
    mixed = jnp.einsum('srhj,rjc->srhc', cache_w, cache_f[:, :, :KV_RANK]) + jnp.einsum('srht,trc->srhc', new_w, new_f[:, :, :KV_RANK])
    mixed = (mixed / total[..., None]).astype(jnp.bfloat16).astype(jnp.float32)
    decode_out = jnp.einsum('srhc,hcv->srhv', mixed, w_uv.astype(jnp.float32)).astype(jnp.bfloat16)
    return (prefill_out, decode_out)
```

```python
import functools

import jax
import jax.numpy as jnp
from jax import lax
from jax.experimental import pallas as pl
from jax.experimental.pallas import tpu as pltpu
from jax.sharding import PartitionSpec as P

KV_RANK = 512
ROPE = 64
NOPE = 128
LOG2E = 1.4426950408889634
LOW = -1e30
MESH = pl.DeviceIdType.MESH


def nt_dot(a, b):
    return lax.dot_general(a, b, (((1,), (1,)), ((), ())), preferred_element_type=jnp.float32)


def nn_dot(a, b):
    return jnp.dot(a, b, preferred_element_type=jnp.float32)


def kernel(
    dims,
    prompt, query, span, w_uk, w_uv, dlat, owner, lengths, hidden, w_down, gain,
    out_p, out_d,
    lat, qv, uk, uv, down, hid, dl, bys, keys, absp, absd, part, parts,
    lat_send, lat_recv, cache_send, cache_recv, swap_send, swap_recv, raw_send, raw_recv, load,
):
    n, nh, nz, ny, own, ppd, steps = dims
    heads = uk.shape[0]
    queries = absp.shape[1]
    chunk = lat.shape[1]
    group = n // nh
    me = lax.axis_index("ctx")
    hx = lax.axis_index("head")
    c = lax.rem(me, 2)
    y = lax.rem(me // 2, ny)
    z = me // (2 * ny)

    def at(zz, yy, cc):
        return (lax.rem(z + zz, nz) * ny + lax.rem(y + yy, ny)) * 2 + lax.rem(c + cc, 2)

    loads = [
        pltpu.make_async_copy(src, dst, load.at[i])
        for i, (src, dst) in enumerate(
            ((prompt, lat.at[me]), (dlat, dl), (hidden, hid), (w_down, down), (query, qv), (w_uk, uk), (w_uv, uv))
        )
    ]
    for copy in loads:
        copy.start()

    barrier = pltpu.get_barrier_semaphore()
    for k in range(1, n):
        pl.semaphore_signal(barrier, inc=1, device_id=(lax.rem(me + k, n), hx), device_id_type=MESH)
    for k in range(1, nh):
        pl.semaphore_signal(barrier, inc=1, device_id=(me, lax.rem(hx + k, nh)), device_id_type=MESH)
    pl.semaphore_wait(barrier, n - 1 + nh - 1)

    sent = []

    def send(shard, target, src=None):
        copy = pltpu.make_async_remote_copy(
            src_ref=lat.at[shard] if src is None else src,
            dst_ref=lat.at[shard],
            send_sem=lat_send.at[len(sent)],
            recv_sem=lat_recv.at[shard],
            device_id=(target, hx),
            device_id_type=MESH,
        )
        copy.start()
        sent.append(copy)

    def arrived(shard):
        pltpu.make_async_remote_copy(
            src_ref=lat.at[shard], dst_ref=lat.at[shard], send_sem=lat_send.at[0],
            recv_sem=lat_recv.at[shard], device_id=(me, hx), device_id_type=MESH,
        ).wait_recv()

    for dy in range(1, ny):
        send(me, at(0, dy, 0), prompt)
    for dz in range(1, nz):
        send(me, at(dz, 0, 0), prompt)
    send(me, at(0, 0, 1), prompt)

    loads[1].wait()
    rows = dl.shape[0]
    to = lax.broadcasted_iota(jnp.int32, (rows, rows), 0)
    of = lax.broadcasted_iota(jnp.int32, (rows, rows), 1)
    pick = (owner[...] == to // ppd) & (to % ppd == of % ppd)
    picked = nn_dot(jnp.where(pick, 1.0, 0.0).astype(jnp.bfloat16), dl[...])
    bys[...] = picked.astype(jnp.bfloat16).reshape(bys.shape)
    slot_in = hx * group + me // nh

    def cache_copy(k):
        target = lax.rem(me + k, n)
        return pltpu.make_async_remote_copy(
            src_ref=bys.at[target], dst_ref=keys.at[slot_in], send_sem=cache_send.at[k],
            recv_sem=cache_recv.at[me // nh], device_id=(target, hx), device_id_type=MESH,
        )

    mine = lax.rem(me, nh) == hx

    @pl.when(mine)
    def _():
        for k in range(1, n):
            cache_copy(k).start()
        keys[slot_in] = bys[me]

    loads[2].wait()
    loads[3].wait()
    part[...] = nn_dot(hid[...], down[...])
    parts[hx] = part[...]

    def raw_copy(k):
        return pltpu.make_async_remote_copy(
            src_ref=part, dst_ref=parts.at[hx], send_sem=raw_send.at[k], recv_sem=raw_recv.at[hx],
            device_id=(me, lax.rem(hx + k, nh)), device_id_type=MESH,
        )

    for k in range(1, nh):
        raw_copy(k).start()

    def absorb(h, _):
        q = qv[h]
        front = nn_dot(q[:, :NOPE], uk[h]).astype(jnp.bfloat16)
        absp[h, :, :KV_RANK] = front[:queries]
        absd[h, :, :KV_RANK] = front[queries:]
        absp[h, :, KV_RANK:] = q[:queries, NOPE:]
        absd[h, :, KV_RANK:] = q[queries:, NOPE:]
        return 0

    loads[4].wait()
    loads[5].wait()
    loads[0].wait()
    per = -(-heads // (nz - 1))
    for dz in range(1, nz):
        shard = at(dz, 0, 0)
        arrived(shard)
        for dy in range(1, ny):
            send(shard, at(0, dy, 0))
        send(shard, at(0, 0, 1))
        lax.fori_loop(min(heads, (dz - 1) * per), min(heads, dz * per), absorb, 0)
    for dz in range(nz):
        for dy in range(1, ny):
            shard = at(dz, dy, 0)
            arrived(shard)
            send(shard, at(0, 0, 1))

    for g in range(group):
        @pl.when(g * nh + hx != me)
        def _(g=g):
            pltpu.make_async_remote_copy(
                src_ref=bys.at[0], dst_ref=keys.at[hx * group + g], send_sem=cache_send.at[0],
                recv_sem=cache_recv.at[g], device_id=(me, hx), device_id_type=MESH,
            ).wait_recv()

    def swap_copy(k, col):
        here = keys.at[pl.ds(col * group, group)]
        return pltpu.make_async_remote_copy(
            src_ref=here, dst_ref=here, send_sem=swap_send.at[k], recv_sem=swap_recv.at[col],
            device_id=(me, lax.rem(hx + k, nh)), device_id_type=MESH,
        )

    for k in range(1, nh):
        swap_copy(k, hx).start()

    for dz in range(nz):
        for dy in range(ny):
            arrived(at(dz, dy, 1))
    loads[6].wait()

    factor = (NOPE + ROPE) ** (-0.5) * LOG2E
    first = span[0] + me * queries
    total = n * chunk
    per_step = max(1, 256 // queries)
    while heads % per_step:
        per_step -= 1
    spot = lax.broadcasted_iota(jnp.int32, (queries, total), 1)
    limit = first + lax.broadcasted_iota(jnp.int32, (queries, total), 0)
    veto = jnp.where(spot <= limit, 0.0, LOW)

    def attend(i, _):
        h0 = i * per_step
        q = absp[pl.ds(h0, per_step)].reshape(per_step * queries, absp.shape[2])
        k = lat[...].reshape(total, lat.shape[2])
        s = nt_dot(q, k).reshape(per_step, queries, total) + veto[None]
        s = s.reshape(per_step * queries, total)
        m = jnp.max(s, axis=1, keepdims=True)
        p = jnp.exp2((s - m) * factor)
        norm = jnp.sum(p, axis=1, keepdims=True)
        mixed = (nn_dot(p.astype(jnp.bfloat16), k[:, :KV_RANK]) / norm).astype(jnp.bfloat16)
        for j in range(per_step):
            o = nn_dot(mixed[j * queries : (j + 1) * queries], uv[h0 + j])
            out_p[h0 + j] = o.astype(jnp.bfloat16)
        return 0

    lax.fori_loop(0, heads // per_step, attend, 0)

    for k in range(1, nh):
        peer = lax.rem(hx + k, nh)
        pltpu.make_async_remote_copy(
            src_ref=part, dst_ref=parts.at[peer], send_sem=raw_send.at[0], recv_sem=raw_recv.at[peer],
            device_id=(me, hx), device_id_type=MESH,
        ).wait_recv()
        swap_copy(0, peer).wait_recv()
    raw = parts[0]
    for k in range(1, nh):
        raw = raw + parts[k]
    front = raw[:, :KV_RANK]
    scaling = lax.rsqrt(jnp.mean(front * front, axis=1, keepdims=True) + 1e-06)
    keys[n, :, :KV_RANK] = (front * scaling * gain[...]).astype(jnp.bfloat16)
    keys[n, :, KV_RANK:] = raw[:, KV_RANK:].astype(jnp.bfloat16)

    block = own * ppd
    news = steps * own
    kcount = (n + 1) * block
    kid = lax.broadcasted_iota(jnp.int32, (news, kcount), 1)
    rid = lax.broadcasted_iota(jnp.int32, (news, kcount), 0)
    place = kid // block
    inside = kid % block
    source = (place % group) * nh + place // group
    slot = inside // ppd
    position = source * ppd + inside % ppd
    length = jnp.zeros_like(kid)
    for r in range(own):
        length = jnp.where(slot == r, lengths[r], length)
    cached_ok = (slot == rid % own) & (position < length)
    new_ok = (inside % own == rid % own) & (inside // own <= rid // own)
    veto_d = jnp.where(jnp.where(place < n, jnp.where(cached_ok, 1, 0), jnp.where(new_ok, 1, 0)) > 0, 0.0, LOW)

    dper = min(heads, 8)

    def attend_d(i, _):
        h0 = i * dper
        q = absd[pl.ds(h0, dper)].reshape(dper * news, absd.shape[2])
        k = keys[...].reshape(kcount, keys.shape[2])
        s = (nt_dot(q, k).reshape(dper, news, kcount) + veto_d[None]).reshape(dper * news, kcount)
        m = jnp.max(s, axis=1, keepdims=True)
        p = jnp.exp2((s - m) * factor)
        norm = jnp.sum(p, axis=1, keepdims=True)
        mixed = (nn_dot(p.astype(jnp.bfloat16), k[:, :KV_RANK]) / norm).astype(jnp.bfloat16)
        for j in range(dper):
            out_d[h0 + j] = nn_dot(mixed[j * news : (j + 1) * news], uv[h0 + j]).astype(jnp.bfloat16)
        return 0

    lax.fori_loop(0, heads // dper, attend_d, 0)

    for copy in sent:
        copy.wait_send()
    for k in range(1, nh):
        raw_copy(k).wait_send()
        swap_copy(k, hx).wait_send()

    @pl.when(mine)
    def _():
        for k in range(1, n):
            cache_copy(k).wait_send()


def body(
    n, nh,
    prompt_latent, prefill_query, span_start, w_uk, w_uv, decode_latent, owner_slot, lengths,
    hidden_new, decode_query, w_down, kv_gain,
):
    heads = w_uk.shape[0]
    queries = prefill_query.shape[0]
    chunk, width = prompt_latent.shape
    steps, own, cols = hidden_new.shape
    requests, ppd, _ = decode_latent.shape
    news = steps * own
    chips = n // 2
    ny = 1
    while ny * ny * 4 <= chips:
        ny *= 2
    nz = chips // ny
    query = jnp.concatenate(
        [prefill_query, decode_query.reshape(news, heads, decode_query.shape[3])], axis=0
    ).transpose(1, 0, 2)
    dlat = decode_latent.reshape(requests * ppd, width)
    owner = jnp.repeat(owner_slot, ppd)[None, :]
    hidden = hidden_new.reshape(news, cols)
    bf = jnp.bfloat16
    hbm = pl.BlockSpec(memory_space=pl.ANY)
    vmem = pl.BlockSpec(memory_space=pltpu.VMEM)
    smem = pl.BlockSpec(memory_space=pltpu.SMEM)
    dma = pltpu.SemaphoreType.DMA
    block = own * ppd
    out_p, out_d = pl.pallas_call(
        functools.partial(kernel, (n, nh, nz, ny, own, ppd, steps)),
        out_shape=(
            jax.ShapeDtypeStruct((heads, queries, w_uv.shape[2]), bf),
            jax.ShapeDtypeStruct((heads, news, w_uv.shape[2]), bf),
        ),
        in_specs=[hbm, hbm, smem, hbm, hbm, hbm, vmem, smem, hbm, hbm, vmem],
        out_specs=(vmem, vmem),
        scratch_shapes=[
            pltpu.VMEM((n, chunk, width), bf),
            pltpu.VMEM(query.shape, bf),
            pltpu.VMEM(w_uk.shape, bf),
            pltpu.VMEM(w_uv.shape, bf),
            pltpu.VMEM(w_down.shape, bf),
            pltpu.VMEM(hidden.shape, bf),
            pltpu.VMEM(dlat.shape, bf),
            pltpu.VMEM((n, block, width), bf),
            pltpu.VMEM((n + 1, block, width), bf),
            pltpu.VMEM((heads, queries, width), bf),
            pltpu.VMEM((heads, news, width), bf),
            pltpu.VMEM((news, width), jnp.float32),
            pltpu.VMEM((nh, news, width), jnp.float32),
            dma((2 * n,)), dma((n,)), dma((n,)), dma((n // nh,)),
            dma((nh,)), dma((nh,)), dma((nh,)), dma((nh,)), dma((7,)),
        ],
        compiler_params=pltpu.CompilerParams(
            collective_id=0, has_side_effects=True, vmem_limit_bytes=56 * 1024 * 1024
        ),
        cost_estimate=pl.CostEstimate(
            flops=2 * heads * queries * n * chunk * (width + KV_RANK),
            bytes_accessed=2 * (w_uk.size + w_uv.size + w_down.size + query.size),
            transcendentals=heads * queries * n * chunk,
        ),
    )(prompt_latent, query, span_start, w_uk, w_uv, dlat, owner, lengths, hidden, w_down, kv_gain[None, :])
    decode_out = out_d.reshape(heads, steps, own, -1).transpose(1, 2, 0, 3)
    return (out_p.transpose(1, 0, 2), decode_out)


def solution(mesh):
    in_specs = (
        P("ctx", None),
        P("ctx", "head", None),
        P(),
        P("head", None, None),
        P("head", None, None),
        P(None, "ctx", None),
        P(),
        P("ctx"),
        P(None, "ctx", "head"),
        P(None, "ctx", "head", None),
        P("head", None),
        P(),
    )
    out_specs = (P("ctx", "head", None), P(None, "ctx", "head", None))
    n, nh = mesh.shape["ctx"], mesh.shape["head"]
    return jax.shard_map(
        functools.partial(body, n, nh), mesh=mesh, in_specs=in_specs, out_specs=out_specs, check_vma=False
    )
```

```python
import functools

import jax
import jax.numpy as jnp
from jax import lax
from jax.experimental import pallas as pl
from jax.experimental.pallas import tpu as pltpu
from jax.sharding import PartitionSpec as P

KV_RANK = 512
ROPE = 64
NOPE = 128
LOG2E = 1.4426950408889634
LOW = -1e30
MESH = pl.DeviceIdType.MESH


def nt_dot(a, b):
    return lax.dot_general(a, b, (((1,), (1,)), ((), ())), preferred_element_type=jnp.float32)


def nn_dot(a, b):
    return jnp.dot(a, b, preferred_element_type=jnp.float32)


def kernel(
    dims,
    prompt, query, dquery, span, w_uk, w_uv, dlat, owner, lengths, hidden, w_down, gain,
    out_p, out_d,
    lat, lat_t, veto, qv, dqv, uk, uv, down, hid, dl, bys, keys, absp, absd, part, parts, top, total, acc,
    lat_send, lat_recv, cache_send, cache_recv, swap_send, swap_recv, raw_send, raw_recv, load,
):
    n, nh, nz, ny, own, ppd, steps = dims
    heads = uk.shape[0]
    queries = absp.shape[1]
    chunk = lat.shape[1]
    group = n // nh
    plane = n // ny
    me = lax.axis_index("ctx")
    hx = lax.axis_index("head")
    c = lax.rem(me, 2)
    y = lax.rem(me // 2, ny)
    z = me // (2 * ny)

    def at(zz, yy, cc):
        return (lax.rem(z + zz, nz) * ny + lax.rem(y + yy, ny)) * 2 + lax.rem(c + cc, 2)

    def place_of(zz, dy, cc):
        return dy * plane + lax.rem(z + zz, nz) * 2 + lax.rem(c + cc, 2)

    loads = [
        pltpu.make_async_copy(src, dst, load.at[i])
        for i, (src, dst) in enumerate(
            (
                (prompt, lat.at[place_of(0, 0, 0)]), (dlat, dl), (hidden, hid), (w_down, down),
                (query, qv), (dquery, dqv), (w_uk, uk), (w_uv, uv),
            )
        )
    ]
    for copy in loads:
        copy.start()

    barrier = pltpu.get_barrier_semaphore()
    for k in range(1, n):
        pl.semaphore_signal(barrier, inc=1, device_id=(lax.rem(me + k, n), hx), device_id_type=MESH)
    for k in range(1, nh):
        pl.semaphore_signal(barrier, inc=1, device_id=(me, lax.rem(hx + k, nh)), device_id_type=MESH)
    pl.semaphore_wait(barrier, n - 1 + nh - 1)

    sent = []

    def send(src, place, target):
        copy = pltpu.make_async_remote_copy(
            src_ref=src, dst_ref=lat.at[place], send_sem=lat_send.at[len(sent)],
            recv_sem=lat_recv.at[place], device_id=(target, hx), device_id_type=MESH,
        )
        copy.start()
        sent.append(copy)

    def arrived(place):
        pltpu.make_async_remote_copy(
            src_ref=lat.at[place], dst_ref=lat.at[place], send_sem=lat_send.at[0],
            recv_sem=lat_recv.at[place], device_id=(me, hx), device_id_type=MESH,
        ).wait_recv()

    for dz in range(1, nz):
        send(prompt, place_of(0, 0, 0), at(dz, 0, 0))
    for dy in range(1, ny):
        send(prompt, place_of(0, ny - dy, 0), at(0, dy, 0))
    send(prompt, place_of(0, 0, 0), at(0, 0, 1))

    loads[1].wait()
    requests = dl.shape[0]
    rows = requests * ppd
    to = lax.broadcasted_iota(jnp.int32, (rows, requests), 0)
    slot_to = (to // (own * ppd)) * own + to % own
    place_to = (to // own) % ppd
    pick = owner[...] == slot_to
    picked = jnp.zeros((rows, dl.shape[2]), jnp.float32)
    flat = dl[...].astype(jnp.float32)
    for p in range(ppd):
        one = jnp.where(pick & (place_to == p), 1.0, 0.0).astype(jnp.bfloat16)
        picked = picked + nn_dot(one, flat[:, p, :].astype(jnp.bfloat16))
    bys[...] = picked.astype(jnp.bfloat16).reshape(bys.shape)
    slot_in = hx * group + me // nh

    def cache_copy(k):
        target = lax.rem(me + k, n)
        return pltpu.make_async_remote_copy(
            src_ref=bys.at[target], dst_ref=keys.at[slot_in], send_sem=cache_send.at[k],
            recv_sem=cache_recv.at[me // nh], device_id=(target, hx), device_id_type=MESH,
        )

    mine = lax.rem(me, nh) == hx

    @pl.when(mine)
    def _():
        for k in range(1, n):
            cache_copy(k).start()
        keys[slot_in] = bys[me]

    loads[2].wait()
    loads[3].wait()
    part[...] = nt_dot(hid[...].reshape(steps * own, hid.shape[2]), down[...])
    parts[hx] = part[...]

    def raw_copy(k):
        return pltpu.make_async_remote_copy(
            src_ref=part, dst_ref=parts.at[hx], send_sem=raw_send.at[k], recv_sem=raw_recv.at[hx],
            device_id=(me, lax.rem(hx + k, nh)), device_id_type=MESH,
        )

    for k in range(1, nh):
        raw_copy(k).start()

    def absorb(h, _):
        for q, out in ((qv[h], absp), (dqv[h], absd)):
            out[h, :, :KV_RANK] = nn_dot(q[:, :NOPE], uk[h]).astype(jnp.bfloat16)
            out[h, :, KV_RANK:] = q[:, NOPE:]
        return 0

    loads[4].wait()
    loads[5].wait()
    loads[6].wait()
    loads[0].wait()
    per = -(-heads // (nz - 1))
    for dz in range(1, nz):
        shard = place_of(dz, 0, 0)
        arrived(shard)
        for dy in range(1, ny):
            send(lat.at[shard], place_of(dz, ny - dy, 0), at(0, dy, 0))
        send(lat.at[shard], shard, at(0, 0, 1))
        lax.fori_loop(min(heads, (dz - 1) * per), min(heads, dz * per), absorb, 0)

    factor = (NOPE + ROPE) ** (-0.5) * LOG2E
    lanes = veto.shape[1]
    per_step = lanes // queries
    ahead = lax.broadcasted_iota(jnp.int32, (chunk, lanes), 1) % queries - lax.broadcasted_iota(
        jnp.int32, (chunk, lanes), 0
    )
    first = span[0] + me * queries
    for dy in range(ny):
        for k in range(plane):
            base = ((k // 2) * ny + lax.rem(y + dy, ny)) * 2 + k % 2
            place = dy * plane + k
            veto[pl.ds(place * chunk, chunk), :] = jnp.where(ahead >= base * chunk - first, 0.0, LOW)

    together = 4 if (heads // per_step) % 4 == 0 else 1
    depth = plane * chunk

    def attend(dy):
        k = lat[dy * plane : (dy + 1) * plane].reshape(depth, lat.shape[2])
        lat_t[...] = k[:, :KV_RANK].T

        def one_round(i, _):
            groups = [i * together + j for j in range(together)]
            scores = []
            for g in groups:
                q = absp[pl.ds(g * per_step, per_step)].reshape(lanes, absp.shape[2])
                k = lat[dy * plane : (dy + 1) * plane].reshape(depth, lat.shape[2])
                scores.append(nt_dot(k, q))
            for g, s in zip(groups, scores):
                s = s + veto[dy * depth : (dy + 1) * depth, :]
                m = jnp.max(s, axis=0, keepdims=True)
                if dy:
                    before = top[g]
                    m = jnp.maximum(m, before)
                p = jnp.exp2((s - m) * factor)
                norm = jnp.sum(p, axis=0, keepdims=True)
                mixed = nn_dot(lat_t[...], p.astype(jnp.bfloat16))
                if dy:
                    fade = jnp.exp2((before - m) * factor)
                    norm = norm + total[g] * fade
                    mixed = mixed + acc[g] * fade
                if dy < ny - 1:
                    top[g] = m
                    total[g] = norm
                    acc[g] = mixed
                else:
                    mixed = (mixed / norm).T.astype(jnp.bfloat16)
                    for j in range(per_step):
                        h = g * per_step + j
                        o = nn_dot(mixed[j * queries : (j + 1) * queries], uv[h])
                        out_p[h] = o.astype(jnp.bfloat16)
            return 0

        lax.fori_loop(0, heads // per_step // together, one_round, 0)

    for dz in range(nz):
        arrived(place_of(dz, 0, 1))
    attend(0)

    for dy in range(1, ny):
        for dz in range(nz):
            shard = place_of(dz, dy, 0)
            arrived(shard)
            send(lat.at[shard], shard, at(0, 0, 1))

    for g in range(group):
        @pl.when(g * nh + hx != me)
        def _(g=g):
            pltpu.make_async_remote_copy(
                src_ref=bys.at[0], dst_ref=keys.at[hx * group + g], send_sem=cache_send.at[0],
                recv_sem=cache_recv.at[g], device_id=(me, hx), device_id_type=MESH,
            ).wait_recv()

    def swap_copy(k, col):
        here = keys.at[pl.ds(col * group, group)]
        return pltpu.make_async_remote_copy(
            src_ref=here, dst_ref=here, send_sem=swap_send.at[k], recv_sem=swap_recv.at[col],
            device_id=(me, lax.rem(hx + k, nh)), device_id_type=MESH,
        )

    for k in range(1, nh):
        swap_copy(k, hx).start()

    loads[7].wait()
    for dy in range(1, ny):
        for dz in range(nz):
            arrived(place_of(dz, dy, 1))
        attend(dy)

    for k in range(1, nh):
        peer = lax.rem(hx + k, nh)
        pltpu.make_async_remote_copy(
            src_ref=part, dst_ref=parts.at[peer], send_sem=raw_send.at[0], recv_sem=raw_recv.at[peer],
            device_id=(me, hx), device_id_type=MESH,
        ).wait_recv()
        swap_copy(0, peer).wait_recv()
    raw = parts[0]
    for k in range(1, nh):
        raw = raw + parts[k]
    front = raw[:, :KV_RANK]
    scaling = lax.rsqrt(jnp.mean(front * front, axis=1, keepdims=True) + 1e-06)
    keys[n, :, :KV_RANK] = (front * scaling * gain[...]).astype(jnp.bfloat16)
    keys[n, :, KV_RANK:] = raw[:, KV_RANK:].astype(jnp.bfloat16)

    block = own * ppd
    news = steps * own
    kcount = (n + 1) * block
    kid = lax.broadcasted_iota(jnp.int32, (news, kcount), 1)
    rid = lax.broadcasted_iota(jnp.int32, (news, kcount), 0)
    place = kid // block
    inside = kid % block
    source = (place % group) * nh + place // group
    slot = inside % own
    position = source * ppd + inside // own
    length = jnp.zeros_like(kid)
    for r in range(own):
        length = jnp.where(slot == r, lengths[r], length)
    cached_ok = position < length
    new_ok = inside // own <= rid // own
    fits = jnp.where(place < n, jnp.where(cached_ok, 1, 0), jnp.where(new_ok, 1, 0))
    veto_d = jnp.where((fits > 0) & (slot == rid % own), 0.0, LOW)

    dper = min(heads, 16)

    def attend_d(i, _):
        h0 = i * dper
        q = absd[pl.ds(h0, dper)].reshape(dper * news, absd.shape[2])
        k = keys[...].reshape(kcount, keys.shape[2])
        s = (nt_dot(q, k).reshape(dper, news, kcount) + veto_d[None]).reshape(dper * news, kcount)
        m = jnp.max(s, axis=1, keepdims=True)
        p = jnp.exp2((s - m) * factor)
        norm = jnp.sum(p, axis=1, keepdims=True)
        mixed = (nn_dot(p.astype(jnp.bfloat16), k[:, :KV_RANK]) / norm).astype(jnp.bfloat16)
        for j in range(dper):
            out_d[h0 + j] = nn_dot(mixed[j * news : (j + 1) * news], uv[h0 + j]).astype(jnp.bfloat16)
        return 0

    lax.fori_loop(0, heads // dper, attend_d, 0)

    for copy in sent:
        copy.wait_send()
    for k in range(1, nh):
        raw_copy(k).wait_send()
        swap_copy(k, hx).wait_send()

    @pl.when(mine)
    def _():
        for k in range(1, n):
            cache_copy(k).wait_send()


def body(
    n, nh,
    prompt_latent, prefill_query, span_start, w_uk, w_uv, decode_latent, owner_slot, lengths,
    hidden_new, decode_query, w_down, kv_gain,
):
    heads = w_uk.shape[0]
    queries = prefill_query.shape[0]
    chunk, width = prompt_latent.shape
    steps, own, cols = hidden_new.shape
    requests, ppd, _ = decode_latent.shape
    news = steps * own
    chips = n // 2
    ny = 1
    while ny * ny * 4 <= chips:
        ny *= 2
    nz = chips // ny
    query = prefill_query.transpose(1, 0, 2)
    dquery = decode_query.reshape(news, heads, decode_query.shape[3]).transpose(1, 0, 2)
    lanes = queries * (256 // queries)
    while lanes > queries and heads % (lanes // queries):
        lanes -= queries
    groups = heads * queries // lanes
    depth = n // ny * chunk
    bf = jnp.bfloat16
    hbm = pl.BlockSpec(memory_space=pl.ANY)
    vmem = pl.BlockSpec(memory_space=pltpu.VMEM)
    smem = pl.BlockSpec(memory_space=pltpu.SMEM)
    dma = pltpu.SemaphoreType.DMA
    block = own * ppd
    out_p, out_d = pl.pallas_call(
        functools.partial(kernel, (n, nh, nz, ny, own, ppd, steps)),
        out_shape=(
            jax.ShapeDtypeStruct((heads, queries, w_uv.shape[2]), bf),
            jax.ShapeDtypeStruct((heads, news, w_uv.shape[2]), bf),
        ),
        in_specs=[hbm, hbm, hbm, smem, hbm, hbm, hbm, vmem, smem, hbm, hbm, vmem],
        out_specs=(vmem, vmem),
        scratch_shapes=[
            pltpu.VMEM((n, chunk, width), bf),
            pltpu.VMEM((KV_RANK, depth), bf),
            pltpu.VMEM((n * chunk, lanes), jnp.float32),
            pltpu.VMEM(query.shape, bf),
            pltpu.VMEM(dquery.shape, bf),
            pltpu.VMEM(w_uk.shape, bf),
            pltpu.VMEM(w_uv.shape, bf),
            pltpu.VMEM((width, cols), bf),
            pltpu.VMEM(hidden_new.shape, bf),
            pltpu.VMEM(decode_latent.shape, bf),
            pltpu.VMEM((n, block, width), bf),
            pltpu.VMEM((n + 1, block, width), bf),
            pltpu.VMEM((heads, queries, width), bf),
            pltpu.VMEM((heads, news, width), bf),
            pltpu.VMEM((news, width), jnp.float32),
            pltpu.VMEM((nh, news, width), jnp.float32),
            pltpu.VMEM((groups, 1, lanes), jnp.float32),
            pltpu.VMEM((groups, 1, lanes), jnp.float32),
            pltpu.VMEM((groups, KV_RANK, lanes), jnp.float32),
            dma((2 * n,)), dma((n,)), dma((n,)), dma((n // nh,)),
            dma((nh,)), dma((nh,)), dma((nh,)), dma((nh,)), dma((8,)),
        ],
        compiler_params=pltpu.CompilerParams(
            collective_id=0, has_side_effects=True, vmem_limit_bytes=56 * 1024 * 1024
        ),
        cost_estimate=pl.CostEstimate(
            flops=2 * heads * queries * n * chunk * (width + KV_RANK),
            bytes_accessed=2 * (w_uk.size + w_uv.size + w_down.size + query.size),
            transcendentals=heads * queries * n * chunk,
        ),
    )(
        prompt_latent, query, dquery, span_start, w_uk, w_uv, decode_latent, owner_slot[None, :], lengths,
        hidden_new, w_down.T, kv_gain[None, :],
    )
    decode_out = out_d.reshape(heads, steps, own, -1).transpose(1, 2, 0, 3)
    return (out_p.transpose(1, 0, 2), decode_out)


def solution(mesh):
    in_specs = (
        P("ctx", None),
        P("ctx", "head", None),
        P(),
        P("head", None, None),
        P("head", None, None),
        P(None, "ctx", None),
        P(),
        P("ctx"),
        P(None, "ctx", "head"),
        P(None, "ctx", "head", None),
        P("head", None),
        P(),
    )
    out_specs = (P("ctx", "head", None), P(None, "ctx", "head", None))
    n, nh = mesh.shape["ctx"], mesh.shape["head"]
    return jax.shard_map(
        functools.partial(body, n, nh), mesh=mesh, in_specs=in_specs, out_specs=out_specs, check_vma=False
    )
```

```python
import functools

import jax
import jax.numpy as jnp
from jax import lax
from jax.experimental import pallas as pl
from jax.experimental.pallas import tpu as pltpu
from jax.sharding import PartitionSpec as P

KV_RANK = 512
ROPE = 64
NOPE = 128
LOG2E = 1.4426950408889634
LOW = -1e30
MESH = pl.DeviceIdType.MESH


def nt_dot(a, b):
    return lax.dot_general(a, b, (((1,), (1,)), ((), ())), preferred_element_type=jnp.float32)


def nn_dot(a, b):
    return jnp.dot(a, b, preferred_element_type=jnp.float32)


def gather(
    dims,
    prompt, query, dquery, w_uk, dlat, owner, hidden, w_down, gain,
    lat, keys, absp, absd,
    qv, dqv, qt, uk, down, hid, dl, bys, part, parts,
    lat_send, lat_recv, cache_send, cache_recv, swap_send, swap_recv, raw_send, raw_recv, load,
):
    n, nh, nz, ny, own, ppd, steps = dims
    heads = uk.shape[0]
    queries = absp.shape[1]
    chunk = lat.shape[1]
    group = n // nh
    me = lax.axis_index("ctx")
    hx = lax.axis_index("head")
    c = lax.rem(me, 2)
    y = lax.rem(me // 2, ny)
    z = me // (2 * ny)

    def at(zz, yy, cc):
        return (lax.rem(z + zz, nz) * ny + lax.rem(y + yy, ny)) * 2 + lax.rem(c + cc, 2)

    loads = [
        pltpu.make_async_copy(src, dst, load.at[i])
        for i, (src, dst) in enumerate(
            (
                (prompt, lat.at[me]), (dlat, dl), (hidden, hid), (w_down, down),
                (query, qv), (dquery, dqv), (w_uk, uk),
            )
        )
    ]
    for copy in loads:
        copy.start()

    barrier = pltpu.get_barrier_semaphore()
    for k in range(1, n):
        pl.semaphore_signal(barrier, inc=1, device_id=(lax.rem(me + k, n), hx), device_id_type=MESH)
    for k in range(1, nh):
        pl.semaphore_signal(barrier, inc=1, device_id=(me, lax.rem(hx + k, nh)), device_id_type=MESH)
    pl.semaphore_wait(barrier, n - 1 + nh - 1)

    sent = []

    def send(src, place, target):
        copy = pltpu.make_async_remote_copy(
            src_ref=src, dst_ref=lat.at[place], send_sem=lat_send.at[len(sent)],
            recv_sem=lat_recv.at[place], device_id=(target, hx), device_id_type=MESH,
        )
        copy.start()
        sent.append(copy)

    def arrived(place):
        pltpu.make_async_remote_copy(
            src_ref=lat.at[place], dst_ref=lat.at[place], send_sem=lat_send.at[0],
            recv_sem=lat_recv.at[place], device_id=(me, hx), device_id_type=MESH,
        ).wait_recv()

    for dz in range(1, nz):
        send(prompt, me, at(dz, 0, 0))
    for dy in range(1, ny):
        send(prompt, me, at(0, dy, 0))
    send(prompt, me, at(0, 0, 1))

    loads[1].wait()
    requests = dl.shape[0]
    rows = requests * ppd
    to = lax.broadcasted_iota(jnp.int32, (rows, requests), 0)
    slot_to = (to // (own * ppd)) * own + to % own
    place_to = (to // own) % ppd
    pick = owner[...] == slot_to
    picked = jnp.zeros((rows, dl.shape[2]), jnp.float32)
    flat = dl[...].astype(jnp.float32)
    for p in range(ppd):
        one = jnp.where(pick & (place_to == p), 1.0, 0.0).astype(jnp.bfloat16)
        picked = picked + nn_dot(one, flat[:, p, :].astype(jnp.bfloat16))
    bys[...] = picked.astype(jnp.bfloat16).reshape(bys.shape)
    slot_in = hx * group + me // nh

    def cache_copy(k):
        target = lax.rem(me + k, n)
        return pltpu.make_async_remote_copy(
            src_ref=bys.at[target], dst_ref=keys.at[slot_in], send_sem=cache_send.at[k],
            recv_sem=cache_recv.at[me // nh], device_id=(target, hx), device_id_type=MESH,
        )

    mine = lax.rem(me, nh) == hx

    @pl.when(mine)
    def _():
        for k in range(1, n):
            cache_copy(k).start()
        keys[slot_in] = bys[me]

    loads[2].wait()
    loads[3].wait()
    part[...] = nt_dot(hid[...].reshape(steps * own, hid.shape[2]), down[...])
    parts[hx] = part[...]

    def raw_copy(k):
        return pltpu.make_async_remote_copy(
            src_ref=part, dst_ref=parts.at[hx], send_sem=raw_send.at[k], recv_sem=raw_recv.at[hx],
            device_id=(me, lax.rem(hx + k, nh)), device_id_type=MESH,
        )

    for k in range(1, nh):
        raw_copy(k).start()

    def absorb(h, _):
        q = qt[h]
        front = nn_dot(q[:, :NOPE], uk[h]).astype(jnp.bfloat16)
        absp[h, :, :KV_RANK] = front[:queries]
        absd[h, :, :KV_RANK] = front[queries:]
        absp[h, :, KV_RANK:] = q[:queries, NOPE:]
        absd[h, :, KV_RANK:] = q[queries:, NOPE:]
        return 0

    loads[4].wait()
    loads[5].wait()

    def turn(i, _):
        at_q = pl.multiple_of(i * 16, 16)
        qt[:, pl.ds(at_q, 16), :] = jnp.swapaxes(qv[pl.ds(at_q, 16)], 0, 1)
        return 0

    lax.fori_loop(0, queries // 16, turn, 0)
    news = steps * own
    qt[:, queries:, :] = jnp.swapaxes(dqv[...].reshape(news, heads, dqv.shape[3]), 0, 1)
    loads[6].wait()
    loads[0].wait()
    per = -(-heads // (nz - 1))
    for dz in range(1, nz):
        shard = at(dz, 0, 0)
        arrived(shard)
        for dy in range(1, ny):
            send(lat.at[shard], shard, at(0, dy, 0))
        send(lat.at[shard], shard, at(0, 0, 1))
        lax.fori_loop(min(heads, (dz - 1) * per), min(heads, dz * per), absorb, 0)
    for dz in range(nz):
        for dy in range(1, ny):
            shard = at(dz, dy, 0)
            arrived(shard)
            send(lat.at[shard], shard, at(0, 0, 1))

    for g in range(group):
        @pl.when(g * nh + hx != me)
        def _(g=g):
            pltpu.make_async_remote_copy(
                src_ref=bys.at[0], dst_ref=keys.at[hx * group + g], send_sem=cache_send.at[0],
                recv_sem=cache_recv.at[g], device_id=(me, hx), device_id_type=MESH,
            ).wait_recv()

    def swap_copy(k, col):
        here = keys.at[pl.ds(col * group, group)]
        return pltpu.make_async_remote_copy(
            src_ref=here, dst_ref=here, send_sem=swap_send.at[k], recv_sem=swap_recv.at[col],
            device_id=(me, lax.rem(hx + k, nh)), device_id_type=MESH,
        )

    for k in range(1, nh):
        swap_copy(k, hx).start()

    for k in range(1, nh):
        peer = lax.rem(hx + k, nh)
        pltpu.make_async_remote_copy(
            src_ref=part, dst_ref=parts.at[peer], send_sem=raw_send.at[0], recv_sem=raw_recv.at[peer],
            device_id=(me, hx), device_id_type=MESH,
        ).wait_recv()
        swap_copy(0, peer).wait_recv()
    raw = parts[0]
    for k in range(1, nh):
        raw = raw + parts[k]
    front = raw[:, :KV_RANK]
    scaling = lax.rsqrt(jnp.mean(front * front, axis=1, keepdims=True) + 1e-06)
    keys[n, :, :KV_RANK] = (front * scaling * gain[...]).astype(jnp.bfloat16)
    keys[n, :, KV_RANK:] = raw[:, KV_RANK:].astype(jnp.bfloat16)

    for dz in range(nz):
        for dy in range(ny):
            arrived(at(dz, dy, 1))
    for copy in sent:
        copy.wait_send()
    for k in range(1, nh):
        raw_copy(k).wait_send()
        swap_copy(k, hx).wait_send()

    @pl.when(mine)
    def _():
        for k in range(1, n):
            cache_copy(k).wait_send()


def attention(
    dims,
    span, lengths, lat, keys, absp, absd, uv,
    out_p, out_d,
    lat_t, veto,
):
    n, nh, own, ppd, steps = dims
    heads, queries, width = absp.shape
    chunk = lat.shape[1]
    total = n * chunk
    group = n // nh
    block = own * ppd
    news = steps * own
    kcount = (n + 1) * block
    factor = (NOPE + ROPE) ** (-0.5) * LOG2E
    lanes = veto.shape[1]
    per_step = lanes // queries
    first = span[0] + lax.axis_index("ctx") * queries

    @pl.when(pl.program_id(0) == 0)
    def _():
        lat_t[...] = lat[...].reshape(total, width)[:, :KV_RANK].T
        spot = lax.broadcasted_iota(jnp.int32, (total, lanes), 0)
        limit = first + lax.broadcasted_iota(jnp.int32, (total, lanes), 1) % queries
        veto[...] = jnp.where(spot <= limit, 0.0, LOW)

    done = []
    scores = []
    for g in range(heads // per_step):
        q = absp[g * per_step : (g + 1) * per_step].reshape(lanes, width)
        scores.append(nt_dot(lat[...].reshape(total, width), q))
    for g, s in enumerate(scores):
        s = s + veto[...]
        m = jnp.max(s, axis=0, keepdims=True)
        p = jnp.exp2((s - m) * factor)
        norm = jnp.sum(p, axis=0, keepdims=True)
        mixed = (nn_dot(lat_t[...], p.astype(jnp.bfloat16)) / norm).T.astype(jnp.bfloat16)
        for j in range(per_step):
            done.append(nn_dot(mixed[j * queries : (j + 1) * queries], uv[g * per_step + j]))
    out_p[...] = jnp.swapaxes(jnp.stack(done), 0, 1).astype(jnp.bfloat16)

    kid = lax.broadcasted_iota(jnp.int32, (news, kcount), 1)
    rid = lax.broadcasted_iota(jnp.int32, (news, kcount), 0)
    place = kid // block
    inside = kid % block
    source = (place % group) * nh + place // group
    slot = inside % own
    position = source * ppd + inside // own
    length = jnp.zeros_like(kid)
    for r in range(own):
        length = jnp.where(slot == r, lengths[r], length)
    cached_ok = position < length
    new_ok = inside // own <= rid // own
    fits = jnp.where(place < n, jnp.where(cached_ok, 1, 0), jnp.where(new_ok, 1, 0))
    veto_d = jnp.where((fits > 0) & (slot == rid % own), 0.0, LOW)

    q = absd[...].reshape(heads * news, width)
    k = keys[...].reshape(kcount, width)
    s = (nt_dot(q, k).reshape(heads, news, kcount) + veto_d[None]).reshape(heads * news, kcount)
    m = jnp.max(s, axis=1, keepdims=True)
    p = jnp.exp2((s - m) * factor)
    norm = jnp.sum(p, axis=1, keepdims=True)
    mixed = (nn_dot(p.astype(jnp.bfloat16), k[:, :KV_RANK]) / norm).astype(jnp.bfloat16)
    done = [nn_dot(mixed[j * news : (j + 1) * news], uv[j]) for j in range(heads)]
    out_d[...] = jnp.swapaxes(jnp.stack(done), 0, 1).astype(jnp.bfloat16).reshape(out_d.shape)


def body(
    n, nh,
    prompt_latent, prefill_query, span_start, w_uk, w_uv, decode_latent, owner_slot, lengths,
    hidden_new, decode_query, w_down, kv_gain,
):
    heads = w_uk.shape[0]
    queries = prefill_query.shape[0]
    chunk, width = prompt_latent.shape
    steps, own, cols = hidden_new.shape
    requests, ppd, _ = decode_latent.shape
    news = steps * own
    chips = n // 2
    ny = 1
    while ny * ny * 4 <= chips:
        ny *= 2
    nz = chips // ny
    bf = jnp.bfloat16
    hbm = pl.BlockSpec(memory_space=pl.ANY)
    vmem = pl.BlockSpec(memory_space=pltpu.VMEM)
    smem = pl.BlockSpec(memory_space=pltpu.SMEM)
    dma = pltpu.SemaphoreType.DMA
    block = own * ppd
    size = prefill_query.shape[2]
    lat, keys, absp, absd = pl.pallas_call(
        functools.partial(gather, (n, nh, nz, ny, own, ppd, steps)),
        out_shape=(
            jax.ShapeDtypeStruct((n, chunk, width), bf),
            jax.ShapeDtypeStruct((n + 1, block, width), bf),
            jax.ShapeDtypeStruct((heads, queries, width), bf),
            jax.ShapeDtypeStruct((heads, news, width), bf),
        ),
        in_specs=[hbm, hbm, hbm, hbm, hbm, vmem, hbm, hbm, vmem],
        out_specs=(vmem, vmem, vmem, vmem),
        scratch_shapes=[
            pltpu.VMEM(prefill_query.shape, bf),
            pltpu.VMEM(decode_query.shape, bf),
            pltpu.VMEM((heads, queries + news, size), bf),
            pltpu.VMEM(w_uk.shape, bf),
            pltpu.VMEM((width, cols), bf),
            pltpu.VMEM(hidden_new.shape, bf),
            pltpu.VMEM(decode_latent.shape, bf),
            pltpu.VMEM((n, block, width), bf),
            pltpu.VMEM((news, width), jnp.float32),
            pltpu.VMEM((nh, news, width), jnp.float32),
            dma((2 * n,)), dma((n,)), dma((n,)), dma((n // nh,)),
            dma((nh,)), dma((nh,)), dma((nh,)), dma((nh,)), dma((7,)),
        ],
        compiler_params=pltpu.CompilerParams(
            collective_id=0, has_side_effects=True, vmem_limit_bytes=40 * 1024 * 1024
        ),
        cost_estimate=pl.CostEstimate(
            flops=2 * heads * (queries + news) * NOPE * KV_RANK + 2 * news * w_down.size,
            bytes_accessed=2 * (w_uk.size + w_down.size + prefill_query.size),
            transcendentals=0,
        ),
    )(
        prompt_latent, prefill_query, decode_query, w_uk, decode_latent, owner_slot[None, :],
        hidden_new, w_down.T, kv_gain[None, :],
    )
    per_call = min(heads, 8)
    lanes = queries * min(per_call, max(1, 256 // queries))
    vdim = w_uv.shape[2]

    def whole(shape):
        return pl.BlockSpec(shape, lambda i: (0,) * len(shape))

    return pl.pallas_call(
        functools.partial(attention, (n, nh, own, ppd, steps)),
        grid=(heads // per_call,),
        out_shape=(
            jax.ShapeDtypeStruct((queries, heads, vdim), bf),
            jax.ShapeDtypeStruct((steps, own, heads, vdim), bf),
        ),
        in_specs=[
            smem, smem, whole(lat.shape), whole(keys.shape),
            pl.BlockSpec((per_call, queries, width), lambda i: (i, 0, 0)),
            pl.BlockSpec((per_call, news, width), lambda i: (i, 0, 0)),
            pl.BlockSpec((per_call, KV_RANK, vdim), lambda i: (i, 0, 0)),
        ],
        out_specs=(
            pl.BlockSpec((queries, per_call, vdim), lambda i: (0, i, 0)),
            pl.BlockSpec((steps, own, per_call, vdim), lambda i: (0, 0, i, 0)),
        ),
        scratch_shapes=[
            pltpu.VMEM((KV_RANK, n * chunk), bf),
            pltpu.VMEM((n * chunk, lanes), jnp.float32),
        ],
        compiler_params=pltpu.CompilerParams(vmem_limit_bytes=56 * 1024 * 1024),
        cost_estimate=pl.CostEstimate(
            flops=2 * heads * queries * n * chunk * (width + KV_RANK),
            bytes_accessed=2 * (w_uv.size + absp.size + lat.size),
            transcendentals=heads * queries * n * chunk,
        ),
    )(span_start, lengths, lat, keys, absp, absd, w_uv)


def solution(mesh):
    in_specs = (
        P("ctx", None),
        P("ctx", "head", None),
        P(),
        P("head", None, None),
        P("head", None, None),
        P(None, "ctx", None),
        P(),
        P("ctx"),
        P(None, "ctx", "head"),
        P(None, "ctx", "head", None),
        P("head", None),
        P(),
    )
    out_specs = (P("ctx", "head", None), P(None, "ctx", "head", None))
    n, nh = mesh.shape["ctx"], mesh.shape["head"]
    return jax.shard_map(
        functools.partial(body, n, nh), mesh=mesh, in_specs=in_specs, out_specs=out_specs, check_vma=False
    )
```

```python
import functools

import jax
import jax.numpy as jnp
from jax import lax
from jax.experimental import pallas as pl
from jax.experimental.pallas import tpu as pltpu
from jax.sharding import PartitionSpec as P

KV_RANK = 512
ROPE = 64
NOPE = 128
LOG2E = 1.4426950408889634
LOW = -1e30
MESH = pl.DeviceIdType.MESH


def nt_dot(a, b):
    return lax.dot_general(a, b, (((1,), (1,)), ((), ())), preferred_element_type=jnp.float32)


def nn_dot(a, b):
    return jnp.dot(a, b, preferred_element_type=jnp.float32)


def gather(
    dims,
    prompt, query, dquery, w_uk, dlat, owner, hidden, w_down, gain,
    lat, keys, absp, absd,
    qv, dqv, qt, uk, down, hid, dl, bys, part, parts,
    lat_send, lat_recv, cache_send, cache_recv, swap_send, swap_recv, raw_send, raw_recv, load,
):
    n, nh, nz, ny, own, ppd, steps = dims
    heads = uk.shape[0]
    queries = absp.shape[1]
    chunk = lat.shape[1]
    group = n // nh
    me = lax.axis_index("ctx")
    hx = lax.axis_index("head")
    c = lax.rem(me, 2)
    y = lax.rem(me // 2, ny)
    z = me // (2 * ny)

    def at(zz, yy, cc):
        return (lax.rem(z + zz, nz) * ny + lax.rem(y + yy, ny)) * 2 + lax.rem(c + cc, 2)

    loads = [
        pltpu.make_async_copy(src, dst, load.at[i])
        for i, (src, dst) in enumerate(
            (
                (prompt, lat.at[me]), (dlat, dl), (hidden, hid), (w_down, down),
                (query, qv), (dquery, dqv), (w_uk, uk),
            )
        )
    ]
    for copy in loads:
        copy.start()

    barrier = pltpu.get_barrier_semaphore()
    for k in range(1, n):
        pl.semaphore_signal(barrier, inc=1, device_id=(lax.rem(me + k, n), hx), device_id_type=MESH)
    for k in range(1, nh):
        pl.semaphore_signal(barrier, inc=1, device_id=(me, lax.rem(hx + k, nh)), device_id_type=MESH)
    pl.semaphore_wait(barrier, n - 1 + nh - 1)

    sent = []

    def send(k, src, shard, target):
        copy = pltpu.make_async_remote_copy(
            src_ref=src, dst_ref=lat.at[shard], send_sem=lat_send.at[k],
            recv_sem=lat_recv.at[shard], device_id=target, device_id_type=MESH,
        )
        copy.start()
        sent.append((k, relay))

    def arrived(shard):
        pltpu.make_async_remote_copy(
            src_ref=lat.at[shard], dst_ref=lat.at[shard], send_sem=lat_send.at[0],
            recv_sem=lat_recv.at[shard], device_id=(me, hx), device_id_type=MESH,
        ).wait_recv()

    first_half = max(1, nz // 2)
    counts = [0, 0]
    relay = 0

    def forward(src, shard, dz, dy, to_y, to_x):
        def push(target):
            send(counts[relay], src, shard, target)
            counts[relay] += 1

        for k in range(1, ny) if to_y else ():
            push((at(0, k, 0), hx))
        for k in range(1, nh) if to_x else ():
            push((me, lax.rem(hx + k, nh)))
        push((at(0, 0, 1), hx))

    def step(dz, dy):
        nonlocal relay
        for relay in (0, 1):
            @pl.when(leads if relay == 0 else jnp.logical_not(leads))
            def _():
                shard = at(dz, dy, 0)
                if dz or dy:
                    arrived(shard)
                src = lat.at[shard] if dz or dy else prompt
                if relay == 0:
                    if not dz and not dy:
                        for k in range(1, nz):
                            send(counts[0], src, shard, (at(k, 0, 0), hx))
                            counts[0] += 1
                    forward(src, shard, dz, dy, dy == 0, dz >= first_half if dy else dz > 0)
                else:
                    forward(src, shard, dz, dy, dy == 0 and dz < first_half, False)

    leads = hx == c
    step(0, 0)

    loads[1].wait()
    requests = dl.shape[0]
    rows = requests * ppd
    to = lax.broadcasted_iota(jnp.int32, (rows, requests), 0)
    slot_to = (to // (own * ppd)) * own + to % own
    place_to = (to // own) % ppd
    pick = owner[...] == slot_to
    picked = jnp.zeros((rows, dl.shape[2]), jnp.float32)
    flat = dl[...].astype(jnp.float32)
    for p in range(ppd):
        one = jnp.where(pick & (place_to == p), 1.0, 0.0).astype(jnp.bfloat16)
        picked = picked + nn_dot(one, flat[:, p, :].astype(jnp.bfloat16))
    bys[...] = picked.astype(jnp.bfloat16).reshape(bys.shape)
    slot_in = hx * group + me // nh

    def cache_copy(k):
        target = lax.rem(me + k, n)
        return pltpu.make_async_remote_copy(
            src_ref=bys.at[target], dst_ref=keys.at[slot_in], send_sem=cache_send.at[k],
            recv_sem=cache_recv.at[me // nh], device_id=(target, hx), device_id_type=MESH,
        )

    mine = lax.rem(me, nh) == hx

    @pl.when(mine)
    def _():
        for k in range(1, n):
            cache_copy(k).start()
        keys[slot_in] = bys[me]

    loads[2].wait()
    loads[3].wait()
    part[...] = nt_dot(hid[...].reshape(steps * own, hid.shape[2]), down[...])
    parts[hx] = part[...]

    def raw_copy(k):
        return pltpu.make_async_remote_copy(
            src_ref=part, dst_ref=parts.at[hx], send_sem=raw_send.at[k], recv_sem=raw_recv.at[hx],
            device_id=(me, lax.rem(hx + k, nh)), device_id_type=MESH,
        )

    for k in range(1, nh):
        raw_copy(k).start()

    def absorb(h, _):
        q = qt[h]
        front = nn_dot(q[:, :NOPE], uk[h]).astype(jnp.bfloat16)
        absp[h, :, :KV_RANK] = front[:queries]
        absd[h, :, :KV_RANK] = front[queries:]
        absp[h, :, KV_RANK:] = q[:queries, NOPE:]
        absd[h, :, KV_RANK:] = q[queries:, NOPE:]
        return 0

    step(1, 0)
    loads[4].wait()
    loads[5].wait()

    def turn(i, _):
        at_q = pl.multiple_of(i * 16, 16)
        qt[:, pl.ds(at_q, 16), :] = jnp.swapaxes(qv[pl.ds(at_q, 16)], 0, 1)
        return 0

    lax.fori_loop(0, queries // 16, turn, 0)
    news = steps * own
    qt[:, queries:, :] = jnp.swapaxes(dqv[...].reshape(news, heads, dqv.shape[3]), 0, 1)
    loads[6].wait()
    loads[0].wait()
    per = -(-heads // max(1, nz - 2))
    for dz in range(2, nz):
        step(dz, 0)
        lax.fori_loop(min(heads, (dz - 2) * per), min(heads, (dz - 1) * per), absorb, 0)
    for dz in range(nz):
        for dy in range(1, ny):
            step(dz, dy)

    for g in range(group):
        @pl.when(g * nh + hx != me)
        def _(g=g):
            pltpu.make_async_remote_copy(
                src_ref=bys.at[0], dst_ref=keys.at[hx * group + g], send_sem=cache_send.at[0],
                recv_sem=cache_recv.at[g], device_id=(me, hx), device_id_type=MESH,
            ).wait_recv()

    def swap_copy(k, col):
        here = keys.at[pl.ds(col * group, group)]
        return pltpu.make_async_remote_copy(
            src_ref=here, dst_ref=here, send_sem=swap_send.at[k], recv_sem=swap_recv.at[col],
            device_id=(me, lax.rem(hx + k, nh)), device_id_type=MESH,
        )

    for k in range(1, nh):
        swap_copy(k, hx).start()

    for k in range(1, nh):
        peer = lax.rem(hx + k, nh)
        pltpu.make_async_remote_copy(
            src_ref=part, dst_ref=parts.at[peer], send_sem=raw_send.at[0], recv_sem=raw_recv.at[peer],
            device_id=(me, hx), device_id_type=MESH,
        ).wait_recv()
        swap_copy(0, peer).wait_recv()
    raw = parts[0]
    for k in range(1, nh):
        raw = raw + parts[k]
    front = raw[:, :KV_RANK]
    scaling = lax.rsqrt(jnp.mean(front * front, axis=1, keepdims=True) + 1e-06)
    keys[n, :, :KV_RANK] = (front * scaling * gain[...]).astype(jnp.bfloat16)
    keys[n, :, KV_RANK:] = raw[:, KV_RANK:].astype(jnp.bfloat16)

    for dz in range(nz):
        for dy in range(ny):
            arrived(at(dz, dy, 1))
    for relay in (0, 1):
        @pl.when(leads if relay == 0 else jnp.logical_not(leads))
        def _():
            for k, role in sent:
                if role == relay:
                    pltpu.make_async_remote_copy(
                        src_ref=prompt, dst_ref=lat.at[me], send_sem=lat_send.at[k],
                        recv_sem=lat_recv.at[me], device_id=(me, hx), device_id_type=MESH,
                    ).wait_send()
    for k in range(1, nh):
        raw_copy(k).wait_send()
        swap_copy(k, hx).wait_send()

    @pl.when(mine)
    def _():
        for k in range(1, n):
            cache_copy(k).wait_send()


def attention(
    dims,
    span, lengths, lat, keys, absp, absd, uv,
    out_p, out_d,
    lat_t, veto, score, weight,
):
    n, nh, own, ppd, steps = dims
    heads, queries, width = absp.shape
    chunk = lat.shape[1]
    total = n * chunk
    group = n // nh
    block = own * ppd
    news = steps * own
    kcount = (n + 1) * block
    factor = (NOPE + ROPE) ** (-0.5) * LOG2E
    lanes = veto.shape[1]
    per_step = lanes // queries
    first = span[0] + lax.axis_index("ctx") * queries

    @pl.when(pl.program_id(0) == 0)
    def _():
        lat_t[...] = lat[...].reshape(total, width)[:, :KV_RANK].T
        ahead = lax.broadcasted_iota(jnp.int32, (chunk, lanes), 1) % queries - lax.broadcasted_iota(
            jnp.int32, (chunk, lanes), 0
        )
        for k in range(n):
            veto[k * chunk : (k + 1) * chunk] = jnp.where(ahead >= k * chunk - first, 0.0, LOW)

    rows = 64
    for g in range(heads // per_step):
        q = absp[g * per_step : (g + 1) * per_step].reshape(lanes, width)
        score[g] = nt_dot(lat[...].reshape(total, width), q)
    done = []
    for g in range(heads // per_step):
        top = jnp.full((8, lanes), LOW, jnp.float32)
        for r in range(0, total, rows):
            x = score[g, r : r + rows] + veto[r : r + rows]
            score[g, r : r + rows] = x
            top = jnp.maximum(top, jnp.max(x.reshape(rows // 8, 8, lanes), axis=0))
        m = jnp.max(top, axis=0, keepdims=True)
        norm = jnp.zeros((8, lanes), jnp.float32)
        for r in range(0, total, rows):
            p = jnp.exp2((score[g, r : r + rows] - m) * factor)
            norm = norm + jnp.sum(p.reshape(rows // 8, 8, lanes), axis=0)
            weight[g, r : r + rows] = p.astype(jnp.bfloat16)
        norm = jnp.sum(norm, axis=0, keepdims=True)
        mixed = (nn_dot(lat_t[...], weight[g]) / norm).T.astype(jnp.bfloat16)
        for j in range(per_step):
            done.append(nn_dot(mixed[j * queries : (j + 1) * queries], uv[g * per_step + j]))
    out_p[...] = jnp.swapaxes(jnp.stack(done), 0, 1).astype(jnp.bfloat16)

    kid = lax.broadcasted_iota(jnp.int32, (news, kcount), 1)
    rid = lax.broadcasted_iota(jnp.int32, (news, kcount), 0)
    place = kid // block
    inside = kid % block
    source = (place % group) * nh + place // group
    slot = inside % own
    position = source * ppd + inside // own
    length = jnp.zeros_like(kid)
    for r in range(own):
        length = jnp.where(slot == r, lengths[r], length)
    cached_ok = position < length
    new_ok = inside // own <= rid // own
    fits = jnp.where(place < n, jnp.where(cached_ok, 1, 0), jnp.where(new_ok, 1, 0))
    veto_d = jnp.where((fits > 0) & (slot == rid % own), 0.0, LOW)

    q = absd[...].reshape(heads * news, width)
    k = keys[...].reshape(kcount, width)
    s = (nt_dot(q, k).reshape(heads, news, kcount) + veto_d[None]).reshape(heads * news, kcount)
    m = jnp.max(s, axis=1, keepdims=True)
    p = jnp.exp2((s - m) * factor)
    norm = jnp.sum(p, axis=1, keepdims=True)
    mixed = (nn_dot(p.astype(jnp.bfloat16), k[:, :KV_RANK]) / norm).astype(jnp.bfloat16)
    done = [nn_dot(mixed[j * news : (j + 1) * news], uv[j]) for j in range(heads)]
    out_d[...] = jnp.swapaxes(jnp.stack(done), 0, 1).astype(jnp.bfloat16).reshape(out_d.shape)


def body(
    n, nh,
    prompt_latent, prefill_query, span_start, w_uk, w_uv, decode_latent, owner_slot, lengths,
    hidden_new, decode_query, w_down, kv_gain,
):
    heads = w_uk.shape[0]
    queries = prefill_query.shape[0]
    chunk, width = prompt_latent.shape
    steps, own, cols = hidden_new.shape
    requests, ppd, _ = decode_latent.shape
    news = steps * own
    chips = n // 2
    ny = 1
    while ny * ny * 4 <= chips:
        ny *= 2
    nz = chips // ny
    bf = jnp.bfloat16
    hbm = pl.BlockSpec(memory_space=pl.ANY)
    vmem = pl.BlockSpec(memory_space=pltpu.VMEM)
    smem = pl.BlockSpec(memory_space=pltpu.SMEM)
    dma = pltpu.SemaphoreType.DMA
    block = own * ppd
    size = prefill_query.shape[2]
    lat, keys, absp, absd = pl.pallas_call(
        functools.partial(gather, (n, nh, nz, ny, own, ppd, steps)),
        out_shape=(
            jax.ShapeDtypeStruct((n, chunk, width), bf),
            jax.ShapeDtypeStruct((n + 1, block, width), bf),
            jax.ShapeDtypeStruct((heads, queries, width), bf),
            jax.ShapeDtypeStruct((heads, news, width), bf),
        ),
        in_specs=[hbm, hbm, hbm, hbm, hbm, vmem, hbm, hbm, vmem],
        out_specs=(vmem, vmem, vmem, vmem),
        scratch_shapes=[
            pltpu.VMEM(prefill_query.shape, bf),
            pltpu.VMEM(decode_query.shape, bf),
            pltpu.VMEM((heads, queries + news, size), bf),
            pltpu.VMEM(w_uk.shape, bf),
            pltpu.VMEM((width, cols), bf),
            pltpu.VMEM(hidden_new.shape, bf),
            pltpu.VMEM(decode_latent.shape, bf),
            pltpu.VMEM((n, block, width), bf),
            pltpu.VMEM((news, width), jnp.float32),
            pltpu.VMEM((nh, news, width), jnp.float32),
            dma((2 * n * nh,)), dma((n,)), dma((n,)), dma((n // nh,)),
            dma((nh,)), dma((nh,)), dma((nh,)), dma((nh,)), dma((7,)),
        ],
        compiler_params=pltpu.CompilerParams(
            collective_id=0, has_side_effects=True, vmem_limit_bytes=60 * 1024 * 1024
        ),
        cost_estimate=pl.CostEstimate(
            flops=2 * heads * (queries + news) * NOPE * KV_RANK + 2 * news * w_down.size,
            bytes_accessed=2 * (w_uk.size + w_down.size + prefill_query.size),
            transcendentals=0,
        ),
    )(
        prompt_latent, prefill_query, decode_query, w_uk, decode_latent, owner_slot[None, :],
        hidden_new, w_down.T, kv_gain[None, :],
    )
    per_call = min(heads, 8)
    lanes = queries * min(per_call, max(1, 256 // queries))
    vdim = w_uv.shape[2]

    def whole(shape):
        return pl.BlockSpec(shape, lambda i: (0,) * len(shape))

    return pl.pallas_call(
        functools.partial(attention, (n, nh, own, ppd, steps)),
        grid=(heads // per_call,),
        out_shape=(
            jax.ShapeDtypeStruct((queries, heads, vdim), bf),
            jax.ShapeDtypeStruct((steps, own, heads, vdim), bf),
        ),
        in_specs=[
            smem, smem, whole(lat.shape), whole(keys.shape),
            pl.BlockSpec((per_call, queries, width), lambda i: (i, 0, 0)),
            pl.BlockSpec((per_call, news, width), lambda i: (i, 0, 0)),
            pl.BlockSpec((per_call, KV_RANK, vdim), lambda i: (i, 0, 0)),
        ],
        out_specs=(
            pl.BlockSpec((queries, per_call, vdim), lambda i: (0, i, 0)),
            pl.BlockSpec((steps, own, per_call, vdim), lambda i: (0, 0, i, 0)),
        ),
        scratch_shapes=[
            pltpu.VMEM((KV_RANK, n * chunk), bf),
            pltpu.VMEM((n * chunk, lanes), jnp.float32),
            pltpu.VMEM((per_call * queries // lanes, n * chunk, lanes), jnp.float32),
            pltpu.VMEM((per_call * queries // lanes, n * chunk, lanes), bf),
        ],
        compiler_params=pltpu.CompilerParams(vmem_limit_bytes=60 * 1024 * 1024),
        cost_estimate=pl.CostEstimate(
            flops=2 * heads * queries * n * chunk * (width + KV_RANK),
            bytes_accessed=2 * (w_uv.size + absp.size + lat.size),
            transcendentals=heads * queries * n * chunk,
        ),
    )(span_start, lengths, lat, keys, absp, absd, w_uv)


def solution(mesh):
    in_specs = (
        P("ctx", None),
        P("ctx", "head", None),
        P(),
        P("head", None, None),
        P("head", None, None),
        P(None, "ctx", None),
        P(),
        P("ctx"),
        P(None, "ctx", "head"),
        P(None, "ctx", "head", None),
        P("head", None),
        P(),
    )
    out_specs = (P("ctx", "head", None), P(None, "ctx", "head", None))
    n, nh = mesh.shape["ctx"], mesh.shape["head"]
    return jax.shard_map(
        functools.partial(body, n, nh), mesh=mesh, in_specs=in_specs, out_specs=out_specs, check_vma=False
    )
```

```python
import functools

import jax
import jax.numpy as jnp
from jax import lax
from jax.experimental import pallas as pl
from jax.experimental.pallas import tpu as pltpu
from jax.sharding import PartitionSpec as P

KV_RANK = 512
ROPE = 64
NOPE = 128
LOG2E = 1.4426950408889634
LOW = -1e30
MESH = pl.DeviceIdType.MESH


def nt_dot(a, b):
    return lax.dot_general(a, b, (((1,), (1,)), ((), ())), preferred_element_type=jnp.float32)


def nn_dot(a, b):
    return jnp.dot(a, b, preferred_element_type=jnp.float32)


def gather(
    dims,
    prompt, query, dquery, w_uk, dlat, owner, hidden, w_down, gain,
    lat, keys, absp, absd,
    qv, dqv, qt, uk, down, hid, dl, bys, part, parts,
    lat_send, lat_recv, cache_send, cache_recv, swap_send, swap_recv, raw_send, raw_recv, load,
):
    n, nh, nz, ny, own, ppd, steps = dims
    heads = uk.shape[0]
    queries = absp.shape[1]
    chunk = lat.shape[1]
    group = n // nh
    me = lax.axis_index("ctx")
    hx = lax.axis_index("head")
    c = lax.rem(me, 2)
    y = lax.rem(me // 2, ny)
    z = me // (2 * ny)

    def at(zz, yy, cc):
        return (lax.rem(z + zz, nz) * ny + lax.rem(y + yy, ny)) * 2 + lax.rem(c + cc, 2)

    loads = [
        pltpu.make_async_copy(src, dst, load.at[i])
        for i, (src, dst) in enumerate(
            (
                (prompt, lat.at[me]), (dlat, dl), (hidden, hid), (w_down, down),
                (query, qv), (dquery, dqv), (w_uk, uk),
            )
        )
    ]
    for copy in loads:
        copy.start()

    barrier = pltpu.get_barrier_semaphore()
    for k in range(1, n):
        pl.semaphore_signal(barrier, inc=1, device_id=(lax.rem(me + k, n), hx), device_id_type=MESH)
    for k in range(1, nh):
        pl.semaphore_signal(barrier, inc=1, device_id=(me, lax.rem(hx + k, nh)), device_id_type=MESH)
    pl.semaphore_wait(barrier, n - 1 + nh - 1)

    sent = []

    def send(k, src, shard, target):
        copy = pltpu.make_async_remote_copy(
            src_ref=src, dst_ref=lat.at[shard], send_sem=lat_send.at[k],
            recv_sem=lat_recv.at[shard], device_id=target, device_id_type=MESH,
        )
        copy.start()
        sent.append((k, relay))

    def arrived(shard):
        pltpu.make_async_remote_copy(
            src_ref=lat.at[shard], dst_ref=lat.at[shard], send_sem=lat_send.at[0],
            recv_sem=lat_recv.at[shard], device_id=(me, hx), device_id_type=MESH,
        ).wait_recv()

    first_half = max(1, nz // 2)
    counts = [0, 0]
    relay = 0

    def forward(src, shard, dz, dy, to_y, to_x):
        def push(target):
            send(counts[relay], src, shard, target)
            counts[relay] += 1

        for k in range(1, ny) if to_y else ():
            push((at(0, k, 0), hx))
        for k in range(1, nh) if to_x else ():
            push((me, lax.rem(hx + k, nh)))
        push((at(0, 0, 1), hx))

    def step(dz, dy):
        nonlocal relay
        for relay in (0, 1):
            @pl.when(leads if relay == 0 else jnp.logical_not(leads))
            def _():
                shard = at(dz, dy, 0)
                if dz or dy:
                    arrived(shard)
                src = lat.at[shard] if dz or dy else prompt
                if relay == 0:
                    if not dz and not dy:
                        for k in range(1, nz):
                            send(counts[0], src, shard, (at(k, 0, 0), hx))
                            counts[0] += 1
                    forward(src, shard, dz, dy, dy == 0, dz >= first_half if dy else dz > 0)
                else:
                    forward(src, shard, dz, dy, dy == 0 and dz < first_half, False)

    leads = hx == c
    step(0, 0)

    loads[1].wait()
    requests = dl.shape[0]
    rows = requests * ppd
    to = lax.broadcasted_iota(jnp.int32, (rows, requests), 0)
    pick = jnp.where(owner[...] == (to // (own * ppd)) * own + to % own, 1.0, 0.0).astype(jnp.bfloat16)
    spread = lax.broadcasted_iota(jnp.int32, (requests, rows), 1) // ppd == lax.broadcasted_iota(
        jnp.int32, (requests, rows), 0
    )
    wide = nn_dot(pick, jnp.where(spread, 1.0, 0.0).astype(jnp.bfloat16))
    place_to = (lax.broadcasted_iota(jnp.int32, (rows, rows), 0) // own) % ppd
    same = lax.broadcasted_iota(jnp.int32, (rows, rows), 1) % ppd == place_to
    wide = jnp.where(same, wide, 0.0).astype(jnp.bfloat16)
    flat = dl[...].astype(jnp.float32).reshape(rows, dl.shape[2]).astype(jnp.bfloat16)
    bys[...] = nn_dot(wide, flat).astype(jnp.bfloat16).reshape(bys.shape)
    slot_in = hx * group + me // nh

    def cache_copy(k):
        target = lax.rem(me + k, n)
        return pltpu.make_async_remote_copy(
            src_ref=bys.at[target], dst_ref=keys.at[slot_in], send_sem=cache_send.at[k],
            recv_sem=cache_recv.at[me // nh], device_id=(target, hx), device_id_type=MESH,
        )

    mine = lax.rem(me, nh) == hx

    @pl.when(mine)
    def _():
        for k in range(1, n):
            cache_copy(k).start()
        keys[slot_in] = bys[me]

    loads[2].wait()
    loads[3].wait()
    part[...] = nt_dot(down[...], hid[...].reshape(steps * own, hid.shape[2])).T
    parts[hx] = part[...]

    def raw_copy(k):
        return pltpu.make_async_remote_copy(
            src_ref=part, dst_ref=parts.at[hx], send_sem=raw_send.at[k], recv_sem=raw_recv.at[hx],
            device_id=(me, lax.rem(hx + k, nh)), device_id_type=MESH,
        )

    for k in range(1, nh):
        raw_copy(k).start()

    news = steps * own
    pair = 2 if heads % 2 == 0 else 1

    def absorb(i, _):
        qs = [qt[i * pair + j] for j in range(pair)]
        lefts = [
            jnp.concatenate([q[:, :NOPE] if k == j else jnp.zeros_like(q[:, :NOPE]) for k in range(pair)], axis=1)
            for j, q in enumerate(qs)
        ]
        right = uk[pl.ds(i * pair, pair)].reshape(pair * NOPE, KV_RANK)
        front = nn_dot(jnp.concatenate(lefts, axis=0), right).astype(jnp.bfloat16)
        for j, q in enumerate(qs):
            h = i * pair + j
            base = j * (queries + news)
            absp[h, :, :KV_RANK] = front[base : base + queries]
            absd[h, :, :KV_RANK] = front[base + queries : base + queries + news]
            absp[h, :, KV_RANK:] = q[:queries, NOPE:]
            absd[h, :, KV_RANK:] = q[queries:, NOPE:]
        return 0

    step(1, 0)
    loads[4].wait()
    loads[5].wait()

    def turn(i, _):
        at_q = pl.multiple_of(i * 16, 16)
        qt[:, pl.ds(at_q, 16), :] = jnp.swapaxes(qv[pl.ds(at_q, 16)], 0, 1)
        return 0

    lax.fori_loop(0, queries // 16, turn, 0)
    qt[:, queries:, :] = jnp.swapaxes(dqv[...].reshape(news, heads, dqv.shape[3]), 0, 1)
    loads[6].wait()
    loads[0].wait()
    pairs = heads // pair
    per = -(-pairs // max(1, nz - 2))
    for dz in range(2, nz):
        step(dz, 0)
        low, high = min(pairs, (dz - 2) * per), min(pairs, (dz - 1) * per)
        if high > low:
            lax.fori_loop(low, high, absorb, 0, unroll=4 if (high - low) % 4 == 0 else 1)
    for dz in range(nz):
        for dy in range(1, ny):
            step(dz, dy)

    for g in range(group):
        @pl.when(g * nh + hx != me)
        def _(g=g):
            pltpu.make_async_remote_copy(
                src_ref=bys.at[0], dst_ref=keys.at[hx * group + g], send_sem=cache_send.at[0],
                recv_sem=cache_recv.at[g], device_id=(me, hx), device_id_type=MESH,
            ).wait_recv()

    def swap_copy(k, col):
        here = keys.at[pl.ds(col * group, group)]
        return pltpu.make_async_remote_copy(
            src_ref=here, dst_ref=here, send_sem=swap_send.at[k], recv_sem=swap_recv.at[col],
            device_id=(me, lax.rem(hx + k, nh)), device_id_type=MESH,
        )

    for k in range(1, nh):
        swap_copy(k, hx).start()

    for k in range(1, nh):
        peer = lax.rem(hx + k, nh)
        pltpu.make_async_remote_copy(
            src_ref=part, dst_ref=parts.at[peer], send_sem=raw_send.at[0], recv_sem=raw_recv.at[peer],
            device_id=(me, hx), device_id_type=MESH,
        ).wait_recv()
        swap_copy(0, peer).wait_recv()
    raw = parts[0]
    for k in range(1, nh):
        raw = raw + parts[k]
    front = raw[:, :KV_RANK]
    scaling = lax.rsqrt(jnp.mean(front * front, axis=1, keepdims=True) + 1e-06)
    keys[n, :, :KV_RANK] = (front * scaling * gain[...]).astype(jnp.bfloat16)
    keys[n, :, KV_RANK:] = raw[:, KV_RANK:].astype(jnp.bfloat16)

    for dz in range(nz):
        for dy in range(ny):
            arrived(at(dz, dy, 1))
    for relay in (0, 1):
        @pl.when(leads if relay == 0 else jnp.logical_not(leads))
        def _():
            for k, role in sent:
                if role == relay:
                    pltpu.make_async_remote_copy(
                        src_ref=prompt, dst_ref=lat.at[me], send_sem=lat_send.at[k],
                        recv_sem=lat_recv.at[me], device_id=(me, hx), device_id_type=MESH,
                    ).wait_send()
    for k in range(1, nh):
        raw_copy(k).wait_send()
        swap_copy(k, hx).wait_send()

    @pl.when(mine)
    def _():
        for k in range(1, n):
            cache_copy(k).wait_send()


def attention(
    dims,
    span, lengths, lat, keys, absp, absd, uv,
    out_p, out_d,
    lat_t, veto, score, weight, veto_d,
):
    n, nh, own, ppd, steps = dims
    heads, queries, width = absp.shape
    chunk = lat.shape[1]
    total = n * chunk
    group = n // nh
    block = own * ppd
    news = steps * own
    kcount = (n + 1) * block
    factor = (NOPE + ROPE) ** (-0.5) * LOG2E
    lanes = veto.shape[1]
    per_step = lanes // queries
    first = span[0] + lax.axis_index("ctx") * queries

    @pl.when(pl.program_id(0) == 0)
    def _():
        lat_t[...] = lat[...].reshape(total, width)[:, :KV_RANK].T
        ahead = lax.broadcasted_iota(jnp.int32, (chunk, lanes), 1) % queries - lax.broadcasted_iota(
            jnp.int32, (chunk, lanes), 0
        )
        for k in range(n):
            veto[k * chunk : (k + 1) * chunk] = jnp.where(ahead >= k * chunk - first, 0.0, LOW)
        kid = lax.broadcasted_iota(jnp.int32, (news, kcount), 1)
        rid = lax.broadcasted_iota(jnp.int32, (news, kcount), 0)
        place = kid // block
        inside = kid % block
        source = (place % group) * nh + place // group
        slot = inside % own
        position = source * ppd + inside // own
        length = jnp.zeros_like(kid)
        for r in range(own):
            length = jnp.where(slot == r, lengths[r], length)
        cached_ok = position < length
        new_ok = inside // own <= rid // own
        fits = jnp.where(place < n, jnp.where(cached_ok, 1, 0), jnp.where(new_ok, 1, 0))
        veto_d[...] = jnp.where((fits > 0) & (slot == rid % own), 0.0, LOW)

    rows = 64
    for g in range(heads // per_step):
        q = absp[g * per_step : (g + 1) * per_step].reshape(lanes, width)
        score[g] = nt_dot(lat[...].reshape(total, width), q)
    q = absd[...].reshape(heads * news, width)
    k = keys[...].reshape(kcount, width)
    s = (nt_dot(q, k).reshape(heads, news, kcount) + veto_d[...][None]).reshape(heads * news, kcount)
    m = jnp.max(s, axis=1, keepdims=True)
    p = jnp.exp2((s - m) * factor)
    norm = jnp.sum(p, axis=1, keepdims=True)
    mixed_d = (nn_dot(p.astype(jnp.bfloat16), k[:, :KV_RANK]) / norm).astype(jnp.bfloat16)
    done, done_d = [], []
    pair = 2 if per_step % 2 == 0 else 1
    for g in range(heads // per_step):
        top = jnp.full((8, lanes), LOW, jnp.float32)
        for r in range(0, total, rows):
            x = score[g, r : r + rows] + veto[r : r + rows]
            score[g, r : r + rows] = x
            top = jnp.maximum(top, jnp.max(x.reshape(rows // 8, 8, lanes), axis=0))
        m = jnp.max(top, axis=0, keepdims=True)
        norm = jnp.zeros((8, lanes), jnp.float32)
        for r in range(0, total, rows):
            p = jnp.exp2((score[g, r : r + rows] - m) * factor)
            norm = norm + jnp.sum(p.reshape(rows // 8, 8, lanes), axis=0)
            weight[g, r : r + rows] = p.astype(jnp.bfloat16)
        norm = jnp.sum(norm, axis=0, keepdims=True)
        mixed = (nn_dot(lat_t[...], weight[g]) / norm).T.astype(jnp.bfloat16)
        for j in range(0, per_step, pair):
            h = g * per_step + j
            left = jnp.concatenate(
                [mixed[j * queries : (j + pair) * queries], mixed_d[h * news : (h + pair) * news]], axis=0
            )
            o = nn_dot(left, jnp.concatenate([uv[h + k] for k in range(pair)], axis=1))
            vdim = uv.shape[2]
            for k in range(pair):
                mine = o[:, k * vdim : (k + 1) * vdim]
                done.append(mine[k * queries : (k + 1) * queries])
                done_d.append(mine[pair * queries + k * news : pair * queries + (k + 1) * news])
    out_p[...] = jnp.swapaxes(jnp.stack(done), 0, 1).astype(jnp.bfloat16)
    out_d[...] = jnp.swapaxes(jnp.stack(done_d), 0, 1).astype(jnp.bfloat16).reshape(out_d.shape)


def body(
    n, nh,
    prompt_latent, prefill_query, span_start, w_uk, w_uv, decode_latent, owner_slot, lengths,
    hidden_new, decode_query, w_down, kv_gain,
):
    heads = w_uk.shape[0]
    queries = prefill_query.shape[0]
    chunk, width = prompt_latent.shape
    steps, own, cols = hidden_new.shape
    requests, ppd, _ = decode_latent.shape
    news = steps * own
    chips = n // 2
    ny = 1
    while ny * ny * 4 <= chips:
        ny *= 2
    nz = chips // ny
    bf = jnp.bfloat16
    hbm = pl.BlockSpec(memory_space=pl.ANY)
    vmem = pl.BlockSpec(memory_space=pltpu.VMEM)
    smem = pl.BlockSpec(memory_space=pltpu.SMEM)
    dma = pltpu.SemaphoreType.DMA
    block = own * ppd
    size = prefill_query.shape[2]
    lat, keys, absp, absd = pl.pallas_call(
        functools.partial(gather, (n, nh, nz, ny, own, ppd, steps)),
        out_shape=(
            jax.ShapeDtypeStruct((n, chunk, width), bf),
            jax.ShapeDtypeStruct((n + 1, block, width), bf),
            jax.ShapeDtypeStruct((heads, queries, width), bf),
            jax.ShapeDtypeStruct((heads, news, width), bf),
        ),
        in_specs=[hbm, hbm, hbm, hbm, hbm, vmem, hbm, hbm, vmem],
        out_specs=(vmem, vmem, vmem, vmem),
        scratch_shapes=[
            pltpu.VMEM(prefill_query.shape, bf),
            pltpu.VMEM(decode_query.shape, bf),
            pltpu.VMEM((heads, queries + news, size), bf),
            pltpu.VMEM(w_uk.shape, bf),
            pltpu.VMEM((width, cols), bf),
            pltpu.VMEM(hidden_new.shape, bf),
            pltpu.VMEM(decode_latent.shape, bf),
            pltpu.VMEM((n, block, width), bf),
            pltpu.VMEM((news, width), jnp.float32),
            pltpu.VMEM((nh, news, width), jnp.float32),
            dma((2 * n * nh,)), dma((n,)), dma((n,)), dma((n // nh,)),
            dma((nh,)), dma((nh,)), dma((nh,)), dma((nh,)), dma((7,)),
        ],
        compiler_params=pltpu.CompilerParams(
            collective_id=0, has_side_effects=True, vmem_limit_bytes=60 * 1024 * 1024
        ),
        cost_estimate=pl.CostEstimate(
            flops=2 * heads * (queries + news) * NOPE * KV_RANK + 2 * news * w_down.size,
            bytes_accessed=2 * (w_uk.size + w_down.size + prefill_query.size),
            transcendentals=0,
        ),
    )(
        prompt_latent, prefill_query, decode_query, w_uk, decode_latent, owner_slot[None, :],
        hidden_new, w_down.T, kv_gain[None, :],
    )
    per_call = min(heads, 8)
    lanes = queries * min(per_call, max(1, 256 // queries))
    vdim = w_uv.shape[2]

    def whole(shape):
        return pl.BlockSpec(shape, lambda i: (0,) * len(shape))

    return pl.pallas_call(
        functools.partial(attention, (n, nh, own, ppd, steps)),
        grid=(heads // per_call,),
        out_shape=(
            jax.ShapeDtypeStruct((queries, heads, vdim), bf),
            jax.ShapeDtypeStruct((steps, own, heads, vdim), bf),
        ),
        in_specs=[
            smem, smem, whole(lat.shape), whole(keys.shape),
            pl.BlockSpec((per_call, queries, width), lambda i: (i, 0, 0)),
            pl.BlockSpec((per_call, news, width), lambda i: (i, 0, 0)),
            pl.BlockSpec((per_call, KV_RANK, vdim), lambda i: (i, 0, 0)),
        ],
        out_specs=(
            pl.BlockSpec((queries, per_call, vdim), lambda i: (0, i, 0)),
            pl.BlockSpec((steps, own, per_call, vdim), lambda i: (0, 0, i, 0)),
        ),
        scratch_shapes=[
            pltpu.VMEM((KV_RANK, n * chunk), bf),
            pltpu.VMEM((n * chunk, lanes), jnp.float32),
            pltpu.VMEM((per_call * queries // lanes, n * chunk, lanes), jnp.float32),
            pltpu.VMEM((per_call * queries // lanes, n * chunk, lanes), bf),
            pltpu.VMEM((news, (n + 1) * block), jnp.float32),
        ],
        compiler_params=pltpu.CompilerParams(vmem_limit_bytes=60 * 1024 * 1024),
        cost_estimate=pl.CostEstimate(
            flops=2 * heads * queries * n * chunk * (width + KV_RANK),
            bytes_accessed=2 * (w_uv.size + absp.size + lat.size),
            transcendentals=heads * queries * n * chunk,
        ),
    )(span_start, lengths, lat, keys, absp, absd, w_uv)


def solution(mesh):
    in_specs = (
        P("ctx", None),
        P("ctx", "head", None),
        P(),
        P("head", None, None),
        P("head", None, None),
        P(None, "ctx", None),
        P(),
        P("ctx"),
        P(None, "ctx", "head"),
        P(None, "ctx", "head", None),
        P("head", None),
        P(),
    )
    out_specs = (P("ctx", "head", None), P(None, "ctx", "head", None))
    n, nh = mesh.shape["ctx"], mesh.shape["head"]
    return jax.shard_map(
        functools.partial(body, n, nh), mesh=mesh, in_specs=in_specs, out_specs=out_specs, check_vma=False
    )
```

```python
import functools

import jax
import jax.numpy as jnp
from jax import lax
from jax.experimental import pallas as pl
from jax.experimental.pallas import tpu as pltpu
from jax.sharding import PartitionSpec as P

KV_RANK = 512
ROPE = 64
NOPE = 128
LOG2E = 1.4426950408889634
LOW = -1e30
MESH = pl.DeviceIdType.MESH


def nt_dot(a, b):
    return lax.dot_general(a, b, (((1,), (1,)), ((), ())), preferred_element_type=jnp.float32)


def nn_dot(a, b):
    return jnp.dot(a, b, preferred_element_type=jnp.float32)


def gather(
    dims,
    prompt, query, dquery, w_uk, dlat, owner, hidden, w_down, gain,
    lat, keys, absp, absd,
    qv, dqv, qt, uk, down, hid, dl, bys, part, parts,
    lat_send, lat_recv, cache_send, cache_recv, swap_send, swap_recv, raw_send, raw_recv, load,
):
    n, nh, nz, ny, own, ppd, steps = dims
    heads = uk.shape[0]
    queries = absp.shape[1]
    chunk = lat.shape[1]
    group = n // nh
    me = lax.axis_index("ctx")
    hx = lax.axis_index("head")
    c = lax.rem(me, 2)
    y = lax.rem(me // 2, ny)
    z = me // (2 * ny)

    def at(zz, yy, cc):
        return (lax.rem(z + zz, nz) * ny + lax.rem(y + yy, ny)) * 2 + lax.rem(c + cc, 2)

    loads = [
        pltpu.make_async_copy(src, dst, load.at[i])
        for i, (src, dst) in enumerate(
            (
                (prompt, lat.at[me]), (dlat, dl), (hidden, hid), (w_down, down),
                (query, qv), (dquery, dqv), (w_uk, uk),
            )
        )
    ]
    for copy in loads:
        copy.start()

    barrier = pltpu.get_barrier_semaphore()
    for k in range(1, n):
        pl.semaphore_signal(barrier, inc=1, device_id=(lax.rem(me + k, n), hx), device_id_type=MESH)
    for k in range(1, nh):
        pl.semaphore_signal(barrier, inc=1, device_id=(me, lax.rem(hx + k, nh)), device_id_type=MESH)
    pl.semaphore_wait(barrier, n - 1 + nh - 1)

    sent = []

    def send(k, src, shard, target):
        copy = pltpu.make_async_remote_copy(
            src_ref=src, dst_ref=lat.at[shard], send_sem=lat_send.at[k],
            recv_sem=lat_recv.at[shard], device_id=target, device_id_type=MESH,
        )
        copy.start()
        sent.append((k, relay))

    def arrived(shard):
        pltpu.make_async_remote_copy(
            src_ref=lat.at[shard], dst_ref=lat.at[shard], send_sem=lat_send.at[0],
            recv_sem=lat_recv.at[shard], device_id=(me, hx), device_id_type=MESH,
        ).wait_recv()

    first_half = max(1, nz // 2)
    counts = [0, 0]
    relay = 0

    def forward(src, shard, dz, dy, to_y, to_x):
        def push(target):
            send(counts[relay], src, shard, target)
            counts[relay] += 1

        for k in range(1, ny) if to_y else ():
            push((at(0, k, 0), hx))
        for k in range(1, nh) if to_x else ():
            push((me, lax.rem(hx + k, nh)))
        push((at(0, 0, 1), hx))

    def step(dz, dy):
        nonlocal relay
        for relay in (0, 1):
            @pl.when(leads if relay == 0 else jnp.logical_not(leads))
            def _():
                shard = at(dz, dy, 0)
                if dz or dy:
                    arrived(shard)
                src = lat.at[shard] if dz or dy else prompt
                if relay == 0:
                    if not dz and not dy:
                        for k in range(1, nz):
                            send(counts[0], src, shard, (at(k, 0, 0), hx))
                            counts[0] += 1
                    forward(src, shard, dz, dy, dy == 0, dz >= first_half if dy else dz > 0)
                else:
                    forward(src, shard, dz, dy, dy == 0 and dz < first_half, False)

    leads = hx == c
    step(0, 0)

    loads[1].wait()
    requests = dl.shape[0]
    rows = requests * ppd
    to = lax.broadcasted_iota(jnp.int32, (rows, requests), 0)
    pick = jnp.where(owner[...] == (to // (own * ppd)) * own + to % own, 1.0, 0.0).astype(jnp.bfloat16)
    spread = lax.broadcasted_iota(jnp.int32, (requests, rows), 1) // ppd == lax.broadcasted_iota(
        jnp.int32, (requests, rows), 0
    )
    wide = nn_dot(pick, jnp.where(spread, 1.0, 0.0).astype(jnp.bfloat16))
    place_to = (lax.broadcasted_iota(jnp.int32, (rows, rows), 0) // own) % ppd
    same = lax.broadcasted_iota(jnp.int32, (rows, rows), 1) % ppd == place_to
    wide = jnp.where(same, wide, 0.0).astype(jnp.bfloat16)
    flat = dl[...].astype(jnp.float32).reshape(rows, dl.shape[2]).astype(jnp.bfloat16)
    bys[...] = nn_dot(wide, flat).astype(jnp.bfloat16).reshape(bys.shape)
    slot_in = hx * group + me // nh

    def cache_copy(k):
        target = lax.rem(me + k, n)
        return pltpu.make_async_remote_copy(
            src_ref=bys.at[target], dst_ref=keys.at[slot_in], send_sem=cache_send.at[k],
            recv_sem=cache_recv.at[me // nh], device_id=(target, hx), device_id_type=MESH,
        )

    mine = lax.rem(me, nh) == hx

    @pl.when(mine)
    def _():
        for k in range(1, n):
            cache_copy(k).start()
        keys[slot_in] = bys[me]

    loads[2].wait()
    loads[3].wait()
    part[...] = nt_dot(down[...], hid[...].reshape(steps * own, hid.shape[2])).T
    parts[hx] = part[...]

    def raw_copy(k):
        return pltpu.make_async_remote_copy(
            src_ref=part, dst_ref=parts.at[hx], send_sem=raw_send.at[k], recv_sem=raw_recv.at[hx],
            device_id=(me, lax.rem(hx + k, nh)), device_id_type=MESH,
        )

    for k in range(1, nh):
        raw_copy(k).start()

    news = steps * own
    pair = 2 if heads % 2 == 0 else 1

    def absorb(i, _):
        qs = [qt[i * pair + j] for j in range(pair)]
        lefts = [
            jnp.concatenate([q[:, :NOPE] if k == j else jnp.zeros_like(q[:, :NOPE]) for k in range(pair)], axis=1)
            for j, q in enumerate(qs)
        ]
        right = uk[pl.ds(i * pair, pair)].reshape(pair * NOPE, KV_RANK)
        front = nn_dot(jnp.concatenate(lefts, axis=0), right).astype(jnp.bfloat16)
        for j, q in enumerate(qs):
            h = i * pair + j
            base = j * (queries + news)
            absp[h, :, :KV_RANK] = front[base : base + queries]
            absd[h, :, :KV_RANK] = front[base + queries : base + queries + news]
            absp[h, :, KV_RANK:] = q[:queries, NOPE:]
            absd[h, :, KV_RANK:] = q[queries:, NOPE:]
        return 0

    step(1, 0)
    loads[4].wait()
    loads[5].wait()

    def turn(i, _):
        at_q = pl.multiple_of(i * 16, 16)
        qt[:, pl.ds(at_q, 16), :] = jnp.swapaxes(qv[pl.ds(at_q, 16)], 0, 1)
        return 0

    half = queries // 32
    lax.fori_loop(0, half, turn, 0)
    for dz in range(2, nz):
        step(dz, 0)
    lax.fori_loop(half, queries // 16, turn, 0)
    qt[:, queries:, :] = jnp.swapaxes(dqv[...].reshape(news, heads, dqv.shape[3]), 0, 1)
    loads[6].wait()
    loads[0].wait()
    pairs = heads // pair

    def absorb_some(k, parts_of):
        low, high = k * pairs // parts_of, (k + 1) * pairs // parts_of
        if high > low:
            lax.fori_loop(low, high, absorb, 0, unroll=4 if (high - low) % 4 == 0 else 1)

    far = [(dz, dy) for dz in range(nz) for dy in range(1, ny)]
    for k, (dz, dy) in enumerate(far):
        step(dz, dy)
        if k < len(far) - 1:
            absorb_some(k, len(far))

    for g in range(group):
        @pl.when(g * nh + hx != me)
        def _(g=g):
            pltpu.make_async_remote_copy(
                src_ref=bys.at[0], dst_ref=keys.at[hx * group + g], send_sem=cache_send.at[0],
                recv_sem=cache_recv.at[g], device_id=(me, hx), device_id_type=MESH,
            ).wait_recv()

    def swap_copy(k, col):
        here = keys.at[pl.ds(col * group, group)]
        return pltpu.make_async_remote_copy(
            src_ref=here, dst_ref=here, send_sem=swap_send.at[k], recv_sem=swap_recv.at[col],
            device_id=(me, lax.rem(hx + k, nh)), device_id_type=MESH,
        )

    for k in range(1, nh):
        swap_copy(k, hx).start()

    absorb_some(len(far) - 1, len(far))
    for k in range(1, nh):
        peer = lax.rem(hx + k, nh)
        pltpu.make_async_remote_copy(
            src_ref=part, dst_ref=parts.at[peer], send_sem=raw_send.at[0], recv_sem=raw_recv.at[peer],
            device_id=(me, hx), device_id_type=MESH,
        ).wait_recv()
        swap_copy(0, peer).wait_recv()
    raw = parts[0]
    for k in range(1, nh):
        raw = raw + parts[k]
    front = raw[:, :KV_RANK]
    scaling = lax.rsqrt(jnp.mean(front * front, axis=1, keepdims=True) + 1e-06)
    keys[n, :, :KV_RANK] = (front * scaling * gain[...]).astype(jnp.bfloat16)
    keys[n, :, KV_RANK:] = raw[:, KV_RANK:].astype(jnp.bfloat16)

    for dz in range(nz):
        for dy in range(ny):
            arrived(at(dz, dy, 1))
    for relay in (0, 1):
        @pl.when(leads if relay == 0 else jnp.logical_not(leads))
        def _():
            for k, role in sent:
                if role == relay:
                    pltpu.make_async_remote_copy(
                        src_ref=prompt, dst_ref=lat.at[me], send_sem=lat_send.at[k],
                        recv_sem=lat_recv.at[me], device_id=(me, hx), device_id_type=MESH,
                    ).wait_send()
    for k in range(1, nh):
        raw_copy(k).wait_send()
        swap_copy(k, hx).wait_send()

    @pl.when(mine)
    def _():
        for k in range(1, n):
            cache_copy(k).wait_send()


def attention(
    dims,
    span, lengths, lat, keys, absp, absd, uv,
    out_p, out_d,
    lat_t, veto, score, weight, veto_d,
):
    n, nh, own, ppd, steps = dims
    heads, queries, width = absp.shape
    chunk = lat.shape[1]
    total = n * chunk
    group = n // nh
    block = own * ppd
    news = steps * own
    kcount = (n + 1) * block
    factor = (NOPE + ROPE) ** (-0.5) * LOG2E
    lanes = veto.shape[1]
    per_step = lanes // queries
    first = span[0] + lax.axis_index("ctx") * queries

    @pl.when(pl.program_id(0) == 0)
    def _():
        lat_t[...] = lat[...].reshape(total, width)[:, :KV_RANK].T
        ahead = lax.broadcasted_iota(jnp.int32, (chunk, lanes), 1) % queries - lax.broadcasted_iota(
            jnp.int32, (chunk, lanes), 0
        )
        for k in range(n):
            veto[k * chunk : (k + 1) * chunk] = jnp.where(ahead >= k * chunk - first, 0.0, LOW)
        kid = lax.broadcasted_iota(jnp.int32, (news, kcount), 1)
        rid = lax.broadcasted_iota(jnp.int32, (news, kcount), 0)
        place = kid // block
        inside = kid % block
        source = (place % group) * nh + place // group
        slot = inside % own
        position = source * ppd + inside // own
        length = jnp.zeros_like(kid)
        for r in range(own):
            length = jnp.where(slot == r, lengths[r], length)
        cached_ok = position < length
        new_ok = inside // own <= rid // own
        fits = jnp.where(place < n, jnp.where(cached_ok, 1, 0), jnp.where(new_ok, 1, 0))
        veto_d[...] = jnp.where((fits > 0) & (slot == rid % own), 0.0, LOW)

    q = absd[...].reshape(heads * news, width)
    k = keys[...].reshape(kcount, width)
    s = (nt_dot(q, k).reshape(heads, news, kcount) + veto_d[...][None]).reshape(heads * news, kcount)
    m = jnp.max(s, axis=1, keepdims=True)
    p = jnp.exp2((s - m) * factor)
    norm = jnp.sum(p, axis=1, keepdims=True)
    mixed_d = (nn_dot(p.astype(jnp.bfloat16), k[:, :KV_RANK]) / norm).astype(jnp.bfloat16)
    def run(depth):
        rows = 64
        for g in range(heads // per_step):
            q = absp[g * per_step : (g + 1) * per_step].reshape(lanes, width)
            score[g, :depth] = nt_dot(lat[...].reshape(total, width)[:depth], q)
        done, done_d = [], []
        pair = 2 if per_step % 2 == 0 else 1
        for g in range(heads // per_step):
            top = jnp.full((8, lanes), LOW, jnp.float32)
            for r in range(0, depth, rows):
                x = score[g, r : r + rows] + veto[r : r + rows]
                score[g, r : r + rows] = x
                top = jnp.maximum(top, jnp.max(x.reshape(rows // 8, 8, lanes), axis=0))
            m = jnp.max(top, axis=0, keepdims=True)
            norm = jnp.zeros((8, lanes), jnp.float32)
            for r in range(0, depth, rows):
                p = jnp.exp2((score[g, r : r + rows] - m) * factor)
                norm = norm + jnp.sum(p.reshape(rows // 8, 8, lanes), axis=0)
                weight[g, r : r + rows] = p.astype(jnp.bfloat16)
            norm = jnp.sum(norm, axis=0, keepdims=True)
            mixed = (nn_dot(lat_t[:, :depth], weight[g, :depth]) / norm).T.astype(jnp.bfloat16)
            for j in range(0, per_step, pair):
                h = g * per_step + j
                left = jnp.concatenate(
                    [mixed[j * queries : (j + pair) * queries], mixed_d[h * news : (h + pair) * news]], axis=0
                )
                o = nn_dot(left, jnp.concatenate([uv[h + k] for k in range(pair)], axis=1))
                vdim = uv.shape[2]
                for k in range(pair):
                    mine = o[:, k * vdim : (k + 1) * vdim]
                    done.append(mine[k * queries : (k + 1) * queries])
                    done_d.append(mine[pair * queries + k * news : pair * queries + (k + 1) * news])
        out_p[...] = jnp.swapaxes(jnp.stack(done), 0, 1).astype(jnp.bfloat16)
        out_d[...] = jnp.swapaxes(jnp.stack(done_d), 0, 1).astype(jnp.bfloat16).reshape(out_d.shape)

    short = total * 5 // 6 // 128 * 128
    enough = first + queries <= short

    @pl.when(enough)
    def _():
        run(short)

    @pl.when(jnp.logical_not(enough))
    def _():
        run(total)


def body(
    n, nh,
    prompt_latent, prefill_query, span_start, w_uk, w_uv, decode_latent, owner_slot, lengths,
    hidden_new, decode_query, w_down, kv_gain,
):
    heads = w_uk.shape[0]
    queries = prefill_query.shape[0]
    chunk, width = prompt_latent.shape
    steps, own, cols = hidden_new.shape
    requests, ppd, _ = decode_latent.shape
    news = steps * own
    chips = n // 2
    ny = 1
    while ny * ny * 4 <= chips:
        ny *= 2
    nz = chips // ny
    bf = jnp.bfloat16
    hbm = pl.BlockSpec(memory_space=pl.ANY)
    vmem = pl.BlockSpec(memory_space=pltpu.VMEM)
    smem = pl.BlockSpec(memory_space=pltpu.SMEM)
    dma = pltpu.SemaphoreType.DMA
    block = own * ppd
    size = prefill_query.shape[2]
    lat, keys, absp, absd = pl.pallas_call(
        functools.partial(gather, (n, nh, nz, ny, own, ppd, steps)),
        out_shape=(
            jax.ShapeDtypeStruct((n, chunk, width), bf),
            jax.ShapeDtypeStruct((n + 1, block, width), bf),
            jax.ShapeDtypeStruct((heads, queries, width), bf),
            jax.ShapeDtypeStruct((heads, news, width), bf),
        ),
        in_specs=[hbm, hbm, hbm, hbm, hbm, vmem, hbm, hbm, vmem],
        out_specs=(vmem, vmem, vmem, vmem),
        scratch_shapes=[
            pltpu.VMEM(prefill_query.shape, bf),
            pltpu.VMEM(decode_query.shape, bf),
            pltpu.VMEM((heads, queries + news, size), bf),
            pltpu.VMEM(w_uk.shape, bf),
            pltpu.VMEM((width, cols), bf),
            pltpu.VMEM(hidden_new.shape, bf),
            pltpu.VMEM(decode_latent.shape, bf),
            pltpu.VMEM((n, block, width), bf),
            pltpu.VMEM((news, width), jnp.float32),
            pltpu.VMEM((nh, news, width), jnp.float32),
            dma((2 * n * nh,)), dma((n,)), dma((n,)), dma((n // nh,)),
            dma((nh,)), dma((nh,)), dma((nh,)), dma((nh,)), dma((7,)),
        ],
        compiler_params=pltpu.CompilerParams(
            collective_id=0, has_side_effects=True, vmem_limit_bytes=60 * 1024 * 1024
        ),
        cost_estimate=pl.CostEstimate(
            flops=2 * heads * (queries + news) * NOPE * KV_RANK + 2 * news * w_down.size,
            bytes_accessed=2 * (w_uk.size + w_down.size + prefill_query.size),
            transcendentals=0,
        ),
    )(
        prompt_latent, prefill_query, decode_query, w_uk, decode_latent, owner_slot[None, :],
        hidden_new, w_down.T, kv_gain[None, :],
    )
    per_call = min(heads, 8)
    lanes = queries * min(per_call, max(1, 256 // queries))
    vdim = w_uv.shape[2]

    def whole(shape):
        return pl.BlockSpec(shape, lambda i: (0,) * len(shape))

    return pl.pallas_call(
        functools.partial(attention, (n, nh, own, ppd, steps)),
        grid=(heads // per_call,),
        out_shape=(
            jax.ShapeDtypeStruct((queries, heads, vdim), bf),
            jax.ShapeDtypeStruct((steps, own, heads, vdim), bf),
        ),
        in_specs=[
            smem, smem, whole(lat.shape), whole(keys.shape),
            pl.BlockSpec((per_call, queries, width), lambda i: (i, 0, 0)),
            pl.BlockSpec((per_call, news, width), lambda i: (i, 0, 0)),
            pl.BlockSpec((per_call, KV_RANK, vdim), lambda i: (i, 0, 0)),
        ],
        out_specs=(
            pl.BlockSpec((queries, per_call, vdim), lambda i: (0, i, 0)),
            pl.BlockSpec((steps, own, per_call, vdim), lambda i: (0, 0, i, 0)),
        ),
        scratch_shapes=[
            pltpu.VMEM((KV_RANK, n * chunk), bf),
            pltpu.VMEM((n * chunk, lanes), jnp.float32),
            pltpu.VMEM((per_call * queries // lanes, n * chunk, lanes), jnp.float32),
            pltpu.VMEM((per_call * queries // lanes, n * chunk, lanes), bf),
            pltpu.VMEM((news, (n + 1) * block), jnp.float32),
        ],
        compiler_params=pltpu.CompilerParams(vmem_limit_bytes=60 * 1024 * 1024),
        cost_estimate=pl.CostEstimate(
            flops=2 * heads * queries * n * chunk * (width + KV_RANK),
            bytes_accessed=2 * (w_uv.size + absp.size + lat.size),
            transcendentals=heads * queries * n * chunk,
        ),
    )(span_start, lengths, lat, keys, absp, absd, w_uv)


def solution(mesh):
    in_specs = (
        P("ctx", None),
        P("ctx", "head", None),
        P(),
        P("head", None, None),
        P("head", None, None),
        P(None, "ctx", None),
        P(),
        P("ctx"),
        P(None, "ctx", "head"),
        P(None, "ctx", "head", None),
        P("head", None),
        P(),
    )
    out_specs = (P("ctx", "head", None), P(None, "ctx", "head", None))
    n, nh = mesh.shape["ctx"], mesh.shape["head"]
    return jax.shard_map(
        functools.partial(body, n, nh), mesh=mesh, in_specs=in_specs, out_specs=out_specs, check_vma=False
    )
```
